512 devices in a mesh: dp: 16 (over y, core), expert: 32 (over z, x).
Axes of the slice: x: 4, y: 8, z: 8, core: 2. Of those that a mesh axis runs over, the one named last changes fastest.
Arguments:
- stream_q: bfloat16 [4096, 4096], P('dp', 'expert'), may hold values from -6 to 6
- stream_k: bfloat16 [4096, 4096], P('dp', 'expert'), may hold values from -6 to 6
- stream_v: bfloat16 [4096, 4096], P('dp', 'expert'), may hold values from -6 to 6
- conv_taps: float32 [3, 3, 4096], P(None, None, 'expert'), may hold values from -14 to 14
- norm_gain: bfloat16 [4096], P('expert'), may hold values from 0.3984375 to 1.59375
- slot_token: int32 [16, 384], P('dp'), may hold values from 0 to 256, as said below
- expert_count: int32 [16, 2], P('dp'), may hold values from 0 to 256, as said below
- route_prob: float32 [4096], P('dp'), may hold values from 0.25 to 1
- w_proj: bfloat16 [4096, 2, 8192], P('dp', None, 'expert'), may hold values from -0.09375 to 0.09375
- grad_out: bfloat16 [4096, 8192], P('dp', 'expert'), may hold values from -0.75 to 0.75
Outputs:
- activation: bfloat16 [4096, 8192], P('dp', 'expert')
- weight_grad: float32 [4096, 2, 8192], P('dp', None, 'expert')
The draws below stay inside these ranges and needn't reach their ends.
Inputs may be any that keep to these rules, and one draw needn't show every extreme that they name: `slot_token`: for each index of dp the slots hold its 256 local token numbers, each exactly once, grouped by expert in expert order; each group starts at a multiple of 128 and is padded with the value 256 up to a multiple of 128; all slots after the last group hold 256. `expert_count`: the size of each expert's group in slot_token, before padding; each row sums to 256.
All inputs are finite; a program needn't handle non-finite values.
Results may differ from the reference program's by a relative error of at most 0.023.
Values may be sent and summed in bfloat16 or wider, within the bound.
No kernel may reach another device: no remote copies, remote signals or barrier semaphores. Data moves between devices by JAX's collectives and lax.ppermute only.
A program may use at most 64 MiB of HBM per device.

```python
import math
import jax
import jax.numpy as jnp
from jax import lax

D = 4096
HID = 8192
EXP_WIN = 2
BLOCK = 128
TOK_DEV = 256
TOKENS = 4096
SLOTS = 384


def route_tables(key):
    shards = TOKENS // TOK_DEV
    key_level, key_pick = jax.random.split(key)
    levels = jax.random.randint(key_level, (shards,), 1, 8)
    levels = levels.at[0].set(8)
    picks = jax.random.randint(key_pick, (shards, TOK_DEV), 0, 8)
    chosen = (picks >= levels[:, None]).astype(jnp.int32)

    def one_device(picked):
        counts = jnp.sum((picked[:, None] == jnp.arange(EXP_WIN, dtype=jnp.int32)[None, :]).astype(jnp.int32), axis=0)
        padded = (counts + BLOCK - 1) // BLOCK * BLOCK
        pad_start = (jnp.cumsum(padded) - padded).astype(jnp.int32)
        raw_start = (jnp.cumsum(counts) - counts).astype(jnp.int32)
        order = jnp.argsort(picked * TOK_DEV + jnp.arange(TOK_DEV, dtype=jnp.int32)).astype(jnp.int32)
        rank_of = jnp.argsort(order).astype(jnp.int32)
        slot_place = (pad_start[picked] + rank_of - raw_start[picked]).astype(jnp.int32)
        table = jnp.full((SLOTS,), TOK_DEV, jnp.int32).at[slot_place].set(jnp.arange(TOK_DEV, dtype=jnp.int32))
        return (table, counts.astype(jnp.int32))
    return jax.vmap(one_device)(chosen)


def draw_slot_token(key, part):
    return route_tables(jax.random.fold_in(key, 11))[0]


def draw_expert_count(key, part):
    return route_tables(jax.random.fold_in(key, 11))[1]


def draw_conv_taps(key, part):
    key_sign, key_lead, key_lag, key_spread = jax.random.split(jax.random.fold_in(key, 5), 4)
    lead = jax.random.uniform(key_lead, (3, D), jnp.float32, 0.8, 1.2)
    lagged = jax.random.uniform(key_lag, (3, 2, D), jnp.float32, -0.6, 0.6)
    signs = jnp.where(jax.random.bernoulli(key_sign, 0.5, (3, D)), 1.0, -1.0).astype(jnp.float32)
    base = jnp.concatenate([(signs * lead)[:, None, :], lagged], axis=1)
    spread = jnp.exp(jax.random.uniform(key_spread, (D,), jnp.float32, 0.0, math.log(10.0 / math.sqrt(3.0))))
    rise = jnp.exp(jnp.arange(D, dtype=jnp.float32) * (0.5 * math.log(3.0) / D))
    factor = jnp.stack([jnp.ones((D,), jnp.float32), jnp.ones((D,), jnp.float32), spread * rise])
    return base * factor[:, None, :]


def shard_levels(rng, extent, cuts, smallest, high):
    factor_of = 1.0
    for position, parts in cuts:
        steps = jax.random.uniform(jax.random.fold_in(jax.random.fold_in(rng, 6), position), (parts,), jnp.float32, smallest / len(cuts), high / len(cuts))
        factor_of = factor_of * jnp.repeat(jnp.exp(steps), extent[position] // parts).reshape((-1,) + (1,) * (len(extent) - 1 - position))
    return factor_of


def gaussian(rng, shape, deviation, most, pieces=(), kind=jnp.bfloat16):
    entries = jax.random.normal(rng, shape, jnp.float32) * deviation
    if len(pieces) > 0:
        entries = shard_levels(rng, shape, pieces, -0.22, 0.18) * entries
    return jnp.clip(entries, min=-most, max=most).astype(kind)


def setup_inputs(seed: int = 0) -> dict:
    seeds = jax.random.split(jax.random.key(seed), 11)
    stream_q = gaussian(seeds[0], (TOKENS, D), 1.0, 6.0, ((0, 16), (1, 32)))
    stream_k = gaussian(seeds[1], (TOKENS, D), 1.0, 6.0, ((0, 16), (1, 32)))
    stream_v = gaussian(seeds[2], (TOKENS, D), 1.0, 6.0, ((0, 16), (1, 32)))
    conv_taps = draw_conv_taps(jax.random.fold_in(seeds[10], 71), 0)
    norm_gain = jnp.clip(1.0 + 0.12 * jax.random.normal(seeds[4], (D,), jnp.float32), 0.3984375, 1.59375).astype(jnp.bfloat16)
    slot_token = draw_slot_token(jax.random.fold_in(seeds[10], 71), 0)
    expert_count = draw_expert_count(jax.random.fold_in(seeds[10], 71), 0)
    route_prob = jnp.clip(jnp.exp(math.log(1.0) - 1.3862944 * jax.random.uniform(seeds[7], (TOKENS,), jnp.float32) ** shard_levels(seeds[7], (TOKENS,), ((0, 16),), -0.2, 0.2)), 0.25, 1.0)
    w_proj = gaussian(seeds[8], (D, EXP_WIN, HID), D ** -0.5, 0.09375, ((0, 16), (2, 32)))
    grad_out = gaussian(seeds[9], (TOKENS, HID), (3.0 * TOKENS ** -0.5), 0.75, ((0, 16), (1, 32)))
    return {"stream_q": stream_q, "stream_k": stream_k, "stream_v": stream_v, "conv_taps": conv_taps, "norm_gain": norm_gain, "slot_token": slot_token, "expert_count": expert_count, "route_prob": route_prob, "w_proj": w_proj, "grad_out": grad_out}


epsilon = 1e-06

def short_conv(stream, taps):
    values = stream.astype(jnp.float32)
    padded = jnp.concatenate([jnp.zeros((2, values.shape[1]), jnp.float32), values], axis=0)
    return taps[0] * values + taps[1] * padded[1:-1] + taps[2] * padded[:-2]

def block_owner(counts, num_blocks):
    padded = (counts + BLOCK - 1) // BLOCK * BLOCK
    ends = jnp.cumsum(padded).astype(jnp.int32)
    starts = jnp.arange(num_blocks, dtype=jnp.int32) * BLOCK
    owner = lax.optimization_barrier(jnp.sum((starts[:, None] >= ends[None, :]).astype(jnp.int32), axis=1))
    return jnp.minimum(owner, counts.shape[0] - 1).astype(jnp.int32)

def reference(stream_q, stream_k, stream_v, conv_taps, norm_gain, slot_token, expert_count, route_prob, w_proj, grad_out):
    conv_q = short_conv(stream_q, conv_taps[0])
    conv_k = short_conv(stream_k, conv_taps[1])
    conv_v = short_conv(stream_v, conv_taps[2])
    mixed = (conv_q * conv_k * conv_v).astype(jnp.bfloat16)
    mixed_f = mixed.astype(jnp.float32)
    inv_rms = lax.rsqrt(lax.optimization_barrier(jnp.mean(mixed_f * mixed_f, axis=1)) + epsilon)
    normed = (mixed_f * inv_rms[:, None] * norm_gain.astype(jnp.float32)).astype(jnp.bfloat16)
    shards = slot_token.shape[0]
    hid_all = w_proj.shape[2]
    experts_all = w_proj.shape[1]
    num_blocks = SLOTS // BLOCK

    def shard_step(total, shard):
        first = (shard * TOK_DEV).astype(jnp.int32)
        rows = lax.dynamic_slice_in_dim(normed, first, TOK_DEV, 0)
        slots = lax.dynamic_index_in_dim(slot_token, shard, 0, keepdims=False)
        counts = lax.dynamic_index_in_dim(expert_count, shard, 0, keepdims=False)
        owner = block_owner(counts, num_blocks)
        padded_rows = jnp.concatenate([rows, jnp.zeros((1, D), jnp.bfloat16)], axis=0)
        x_blocks = padded_rows[slots].reshape(num_blocks, BLOCK, D)

        def one_block(pair):
            block_rows, block_owner_id = pair
            weight = lax.dynamic_index_in_dim(w_proj, block_owner_id, 1, keepdims=False)
            return jnp.dot(block_rows, weight, preferred_element_type=jnp.float32)
        pre_act = lax.map(one_block, (x_blocks, owner)).reshape(SLOTS, hid_all)
        probs = lax.dynamic_slice_in_dim(route_prob, first, TOK_DEV, 0)
        slot_prob = jnp.concatenate([probs, jnp.zeros((1,), jnp.float32)])[slots][:, None]
        sigmoid_z = jax.nn.sigmoid(pre_act)
        hidden = (slot_prob * pre_act * sigmoid_z).astype(jnp.bfloat16)
        act_rows = jnp.zeros((TOK_DEV + 1, hid_all), jnp.bfloat16).at[slots].set(hidden)[:TOK_DEV]
        grads = lax.dynamic_slice_in_dim(grad_out, first, TOK_DEV, 0)
        slot_grad = jnp.concatenate([grads, jnp.zeros((1, hid_all), jnp.bfloat16)], axis=0)[slots].astype(jnp.float32)
        grad_pre = (slot_grad * slot_prob * sigmoid_z * (1.0 + pre_act * (1.0 - sigmoid_z))).astype(jnp.bfloat16)
        grad_blocks = grad_pre.reshape(num_blocks, BLOCK, hid_all)

        def add_block(block_id, partial_value):
            term = jnp.dot(x_blocks[block_id].T, grad_blocks[block_id], preferred_element_type=jnp.float32)
            current = lax.dynamic_index_in_dim(partial_value, owner[block_id], 1, keepdims=False)
            return lax.dynamic_update_index_in_dim(partial_value, current + term, owner[block_id], 1)
        partial_value = lax.fori_loop(0, num_blocks, add_block, jnp.zeros((D, experts_all, hid_all), jnp.float32))
        rounded = lax.optimization_barrier(partial_value.astype(jnp.bfloat16))
        return (total + rounded.astype(jnp.float32), act_rows)
    weight_grad, acts = lax.scan(shard_step, jnp.zeros((D, experts_all, hid_all), jnp.float32), jnp.arange(shards, dtype=jnp.int32))
    activation = acts.reshape(shards * TOK_DEV, hid_all)
    return (activation, weight_grad)
```

```python
import functools

import jax
import jax.numpy as jnp
from jax import lax
from jax.experimental import pallas as pl
from jax.experimental.pallas import tpu as pltpu
from jax.sharding import PartitionSpec as P

D = 4096
BLOCK = 128
EPS = 1e-06
NZ, NX, NY = 8, 4, 8
TOK, CH, HID = 256, 128, 256
ROWS = TOK + 16
VMEM_LIMIT = 48 * 1024 * 1024
AXES = ("dp", "expert")
Z_GROUPS = [[z * NX + x for z in range(NZ)] for x in range(NX)]


def shift_x(value, steps):
    pairs = [
        (d * NZ * NX + z * NX + x, d * NZ * NX + z * NX + (x + steps) % NX)
        for d in range(2 * NY)
        for z in range(NZ)
        for x in range(NX)
    ]
    return lax.ppermute(value, AXES, pairs)


def to_row_block(value):
    pairs = [
        (i * NZ * NX + j, (j // 2) * NZ * NX + 2 * i + j % 2)
        for i in range(2 * NY)
        for j in range(NZ * NX)
    ]
    return lax.ppermute(value, AXES, pairs)


def gather_expert(copies):
    n, r, c = copies.shape
    b = lax.all_to_all(
        copies.reshape(n * r, c), "expert", 0, 0, axis_index_groups=Z_GROUPS, tiled=True
    ).reshape(n, r, c)
    low, high = b[: n // 2], b[n // 2 :]
    return (b, shift_x(b, 1), shift_x(b, -1), shift_x(low, 2), shift_x(high, -2))


def gathered_blocks(x_ref, parts):
    own, from_left, from_right, low, high = parts
    x = x_ref[0]
    for ref, off, z0 in (
        (own, 0, 0),
        (from_left, NX - 1, 0),
        (from_right, 1, 0),
        (low, 2, 0),
        (high, 2, NZ // 2),
    ):
        xx = lax.rem(x + off, NX)
        for k in range(ref.shape[0]):
            yield ref, k, (z0 + k) * NX + xx


def mix_kernel(q_ref, k_ref, v_ref, halo_ref, taps_ref, gain_ref, x1_ref, x2_ref):
    prod = None
    row = lax.broadcasted_iota(jnp.int32, (TOK, CH), 0)
    for s, ref in enumerate((q_ref, k_ref, v_ref)):
        cur = ref[...].astype(jnp.float32)
        h0 = halo_ref[s, 0:1, :].astype(jnp.float32)
        h1 = halo_ref[s, 1:2, :].astype(jnp.float32)
        lag1 = jnp.where(row == 0, h1, pltpu.roll(cur, 1, 0))
        lag2 = jnp.where(row == 0, h0, jnp.where(row == 1, h1, pltpu.roll(cur, 2, 0)))
        conv = (
            taps_ref[s, 0:1, :] * cur + taps_ref[s, 1:2, :] * lag1 + taps_ref[s, 2:3, :] * lag2
        )
        prod = conv if prod is None else prod * conv
    mixed = prod.astype(jnp.bfloat16)
    gain = gain_ref[...].astype(jnp.float32)
    tail = jnp.broadcast_to(gain, (16, CH)).astype(jnp.bfloat16)
    for n in range(NZ):
        x1_ref[n, 0:TOK, :] = mixed
        x1_ref[n, TOK:ROWS, :] = tail
    scaled = mixed.astype(jnp.float32) * gain
    x2_ref[...] = scaled.T.astype(jnp.bfloat16)


def forward_kernel(
    x_ref, count_ref, *refs
):
    parts = refs[:5]
    w_ref, g_ref, prob_ref, slot_ref, act_ref, gm_ref, xn_ref = refs[5:]
    square = jnp.zeros((TOK, CH), jnp.float32)
    for ref, k, j in gathered_blocks(x_ref, parts):
        m = ref[k, 0:TOK, :].astype(jnp.float32)
        gain = ref[k, TOK : TOK + 16, :].astype(jnp.float32)[0:1, :]
        square = square + m * m
        xn_ref[:, pl.ds(pl.multiple_of(j * CH, CH), CH)] = (m * gain).astype(jnp.bfloat16)
    inv = lax.rsqrt(jnp.sum(square, axis=1, keepdims=True) / D + EPS)
    both = jnp.dot(xn_ref[...], w_ref[...], preferred_element_type=jnp.float32)
    first = (count_ref[0, 0] + BLOCK - 1) // BLOCK * BLOCK
    slots = slot_ref.shape[1]
    tok = lax.broadcasted_iota(jnp.int32, (TOK, slots), 0)
    place = lax.broadcasted_iota(jnp.int32, (TOK, slots), 1)
    hit = jnp.where((slot_ref[...] == tok) & (place >= first), 1.0, 0.0)
    second = jnp.sum(hit, axis=1, keepdims=True) > 0.5
    r = lax.broadcasted_iota(jnp.int32, (TOK, TOK), 0)
    c = lax.broadcasted_iota(jnp.int32, (TOK, TOK), 1)
    prob = jnp.sum(jnp.where(r == c, prob_ref[...], 0.0), axis=1, keepdims=True)
    pre = jnp.where(second, both[:, HID:], both[:, :HID]) * inv
    sig = jax.nn.sigmoid(pre)
    act_ref[...] = (prob * pre * sig).astype(jnp.bfloat16)
    grad = g_ref[...].astype(jnp.float32) * prob * sig * (1.0 + pre * (1.0 - sig)) * inv
    gm_ref[:, :HID] = jnp.where(second, 0.0, grad).astype(jnp.bfloat16)
    gm_ref[:, HID:] = jnp.where(second, grad, 0.0).astype(jnp.bfloat16)


def weight_kernel(x_ref, *refs):
    parts = refs[:5]
    gm_ref, out_ref, xt_ref = refs[5:]
    for ref, k, j in gathered_blocks(x_ref, parts):
        half = lax.rem(j, 2)
        i = lax.div(j, 2)
        xt_ref[
            pl.ds(pl.multiple_of(half * CH, CH), CH), pl.ds(pl.multiple_of(i * TOK, TOK), TOK)
        ] = ref[k]
    out_ref[...] = jnp.dot(xt_ref[...], gm_ref[...], preferred_element_type=jnp.float32)


def vm(n):
    return [pl.BlockSpec(memory_space=pltpu.VMEM)] * n


def sm(n):
    return [pl.BlockSpec(memory_space=pltpu.SMEM)] * n


def on_device(
    stream_q,
    stream_k,
    stream_v,
    conv_taps,
    norm_gain,
    slot_token,
    expert_count,
    route_prob,
    w_proj,
    grad_out,
):
    params = pltpu.CompilerParams(vmem_limit_bytes=VMEM_LIMIT)
    bf, f32 = jnp.bfloat16, jnp.float32
    w_all = lax.all_gather(w_proj.reshape(TOK, 2 * HID), "dp", axis=0, tiled=True)
    last = jnp.stack([stream_q[-2:], stream_k[-2:], stream_v[-2:]])
    halo = lax.ppermute(last, "dp", [(s, s + 1) for s in range(2 * NY - 1)])
    x1, x2 = pl.pallas_call(
        mix_kernel,
        out_shape=(
            jax.ShapeDtypeStruct((NZ, ROWS, CH), bf),
            jax.ShapeDtypeStruct((CH, TOK), bf),
        ),
        in_specs=vm(6),
        out_specs=tuple(vm(2)),
        compiler_params=params,
    )(stream_q, stream_k, stream_v, halo, conv_taps, norm_gain.reshape(1, CH))
    x_pos = lax.rem(lax.axis_index("expert"), NX).astype(jnp.int32).reshape(1)
    x1_parts = gather_expert(x1)
    activation, gm = pl.pallas_call(
        forward_kernel,
        out_shape=(
            jax.ShapeDtypeStruct((TOK, HID), bf),
            jax.ShapeDtypeStruct((TOK, 2 * HID), bf),
        ),
        in_specs=sm(2) + vm(9),
        out_specs=tuple(vm(2)),
        scratch_shapes=[pltpu.VMEM((TOK, D), bf)],
        compiler_params=params,
    )(
        x_pos,
        expert_count,
        *x1_parts,
        w_all,
        grad_out,
        route_prob.reshape(1, TOK),
        slot_token,
    )
    gm_all = lax.all_gather(gm, "dp", axis=0, tiled=True)
    x2 = to_row_block(x2)
    x2, _ = lax.optimization_barrier((x2, gm))
    x2_parts = gather_expert(jnp.broadcast_to(x2[None], (NZ, CH, TOK)))
    grad_w = pl.pallas_call(
        weight_kernel,
        out_shape=jax.ShapeDtypeStruct((TOK, 2 * HID), f32),
        in_specs=sm(1) + vm(6),
        out_specs=pl.BlockSpec(memory_space=pltpu.VMEM),
        scratch_shapes=[pltpu.VMEM((2 * CH, D), bf)],
        compiler_params=params,
    )(x_pos, *x2_parts, gm_all)
    return activation, grad_w.reshape(TOK, 2, HID)


def solution(mesh):
    placed = (
        P("dp", "expert"),
        P("dp", "expert"),
        P("dp", "expert"),
        P(None, None, "expert"),
        P("expert"),
        P("dp", None),
        P("dp", None),
        P("dp"),
        P("dp", None, "expert"),
        P("dp", "expert"),
    )
    return jax.shard_map(
        on_device,
        mesh=mesh,
        in_specs=placed,
        out_specs=(P("dp", "expert"), P("dp", None, "expert")),
        check_vma=False,
    )
```

```python
import functools

import jax
import jax.numpy as jnp
from jax import lax
from jax.experimental import pallas as pl
from jax.experimental.pallas import tpu as pltpu
from jax.sharding import PartitionSpec as P

D = 4096
BLOCK = 128
EPS = 1e-06
NZ, NX, NY = 8, 4, 8
TOK, CH, HID = 256, 128, 256
ROWS = TOK + 16
VMEM_LIMIT = 48 * 1024 * 1024
AXES = ("dp", "expert")
Z_GROUPS = [[z * NX + x for z in range(NZ)] for x in range(NX)]


def shift_x(value, steps):
    pairs = [
        (d * NZ * NX + z * NX + x, d * NZ * NX + z * NX + (x + steps) % NX)
        for d in range(2 * NY)
        for z in range(NZ)
        for x in range(NX)
    ]
    return lax.ppermute(value, AXES, pairs)


def to_row_block(value):
    pairs = [
        (i * NZ * NX + j, (j // 2) * NZ * NX + 2 * i + j % 2)
        for i in range(2 * NY)
        for j in range(NZ * NX)
    ]
    return lax.ppermute(value, AXES, pairs)


def spread_z(copies):
    n, r, c = copies.shape
    return lax.all_to_all(
        copies.reshape(n * r, c), "expert", 0, 0, axis_index_groups=Z_GROUPS, tiled=True
    ).reshape(n, r, c)


def spread_x(b):
    half = b.shape[0] // 2
    return (b, shift_x(b, 1), shift_x(b, -1), shift_x(b[:half], 2), shift_x(b[half:], -2))


def gathered_blocks(x_ref, parts):
    own, from_left, from_right, low, high = parts
    x = x_ref[0]
    for ref, off, z0 in (
        (own, 0, 0),
        (from_left, NX - 1, 0),
        (from_right, 1, 0),
        (low, 2, 0),
        (high, 2, NZ // 2),
    ):
        xx = lax.rem(x + off, NX)
        for k in range(ref.shape[0]):
            yield ref, k, (z0 + k) * NX + xx


def load_all(pairs, sems):
    copies = [pltpu.make_async_copy(src, dst, sems.at[n]) for n, (src, dst) in enumerate(pairs)]
    for copy in copies:
        copy.start()
    return copies


def pack_kernel(q_ref, k_ref, v_ref, out_ref, sems):
    last = pl.ds(TOK - 16, 16)
    for copy in load_all(
        [(r.at[last], out_ref.at[s]) for s, r in enumerate((q_ref, k_ref, v_ref))], sems
    ):
        copy.wait()


def mix_kernel(
    q_hbm, k_hbm, v_hbm, taps_hbm, gain_hbm, halo_ref, x1_ref, x2_ref,
    q_ref, k_ref, v_ref, taps_ref, gain_ref, sems,
):
    for copy in load_all(
        [
            (q_hbm, q_ref),
            (k_hbm, k_ref),
            (v_hbm, v_ref),
            (taps_hbm, taps_ref),
            (gain_hbm, gain_ref),
        ],
        sems,
    ):
        copy.wait()
    prod = None
    row = lax.broadcasted_iota(jnp.int32, (TOK, CH), 0)
    for s, ref in enumerate((q_ref, k_ref, v_ref)):
        cur = ref[...].astype(jnp.float32)
        before = halo_ref[s].astype(jnp.float32)
        h0, h1 = before[14:15, :], before[15:16, :]
        lag1 = jnp.where(row == 0, h1, pltpu.roll(cur, 1, 0))
        lag2 = jnp.where(row == 0, h0, jnp.where(row == 1, h1, pltpu.roll(cur, 2, 0)))
        conv = (
            taps_ref[s, 0:1, :] * cur + taps_ref[s, 1:2, :] * lag1 + taps_ref[s, 2:3, :] * lag2
        )
        prod = conv if prod is None else prod * conv
    mixed = prod.astype(jnp.bfloat16)
    gain = gain_ref[...].astype(jnp.float32)
    tail = jnp.broadcast_to(gain, (16, CH)).astype(jnp.bfloat16)
    for n in range(NZ):
        x1_ref[n, 0:TOK, :] = mixed
        x1_ref[n, TOK:ROWS, :] = tail
    scaled = mixed.astype(jnp.float32) * gain
    x2_ref[...] = scaled.T.astype(jnp.bfloat16)


def forward_kernel(x_ref, *refs):
    parts = refs[:5]
    sources, (act_ref, gm_ref, xn_ref) = refs[5:10], refs[10:13]
    held, sems = refs[13:18], refs[18]
    g_ref, prob_ref, slot_ref, count_ref, w_ref = held
    copies = load_all(list(zip(sources, held)), sems)
    square = jnp.zeros((TOK, CH), jnp.float32)
    for ref, k, j in gathered_blocks(x_ref, parts):
        m = ref[k, 0:TOK, :].astype(jnp.float32)
        gain = ref[k, TOK : TOK + 16, :].astype(jnp.float32)[0:1, :]
        square = square + m * m
        xn_ref[:, pl.ds(pl.multiple_of(j * CH, CH), CH)] = (m * gain).astype(jnp.bfloat16)
    inv = lax.rsqrt(jnp.sum(square, axis=1, keepdims=True) / D + EPS)
    for copy in copies:
        copy.wait()
    both = jnp.dot(xn_ref[...], w_ref[...], preferred_element_type=jnp.float32)
    first = (count_ref[0:1, 0:1] + BLOCK - 1) // BLOCK * BLOCK
    slots = slot_ref.shape[1]
    tok = lax.broadcasted_iota(jnp.int32, (TOK, slots), 0)
    place = lax.broadcasted_iota(jnp.int32, (TOK, slots), 1)
    hit = jnp.where((slot_ref[...] == tok) & (place >= first), 1.0, 0.0)
    second = jnp.sum(hit, axis=1, keepdims=True) > 0.5
    r = lax.broadcasted_iota(jnp.int32, (TOK, TOK), 0)
    c = lax.broadcasted_iota(jnp.int32, (TOK, TOK), 1)
    prob = jnp.sum(jnp.where(r == c, prob_ref[...], 0.0), axis=1, keepdims=True)
    pre = jnp.where(second, both[:, HID:], both[:, :HID]) * inv
    sig = jax.nn.sigmoid(pre)
    act_ref[...] = (prob * pre * sig).astype(jnp.bfloat16)
    grad = g_ref[...].astype(jnp.float32) * prob * sig * (1.0 + pre * (1.0 - sig)) * inv
    gm_ref[:, :HID] = jnp.where(second, 0.0, grad).astype(jnp.bfloat16)
    gm_ref[:, HID:] = jnp.where(second, grad, 0.0).astype(jnp.bfloat16)


def weight_kernel(x_ref, *refs):
    parts = refs[:5]
    gm_hbm, out_ref, xt_ref, gm_ref, sems = refs[5:]
    copies = load_all([(gm_hbm, gm_ref)], sems)
    for ref, k, j in gathered_blocks(x_ref, parts):
        half = lax.rem(j, 2)
        i = lax.div(j, 2)
        xt_ref[
            pl.ds(pl.multiple_of(half * CH, CH), CH), pl.ds(pl.multiple_of(i * TOK, TOK), TOK)
        ] = ref[k]
    for copy in copies:
        copy.wait()
    out_ref[...] = jnp.dot(xt_ref[...], gm_ref[...], preferred_element_type=jnp.float32)


def vm(n):
    return [pl.BlockSpec(memory_space=pltpu.VMEM)] * n


def hbm(n):
    return [pl.BlockSpec(memory_space=pltpu.HBM)] * n


def sm(n):
    return [pl.BlockSpec(memory_space=pltpu.SMEM)] * n


def on_device(
    stream_q,
    stream_k,
    stream_v,
    conv_taps,
    norm_gain,
    slot_token,
    expert_count,
    route_prob,
    w_proj,
    grad_out,
):
    params = pltpu.CompilerParams(vmem_limit_bytes=VMEM_LIMIT)
    full = pltpu.CompilerParams(vmem_limit_bytes=56 * 1024 * 1024)
    bf, f32 = jnp.bfloat16, jnp.float32
    halo = pl.pallas_call(
        pack_kernel,
        out_shape=jax.ShapeDtypeStruct((3, 16, CH), bf),
        in_specs=hbm(3),
        out_specs=vm(1)[0],
        scratch_shapes=[pltpu.SemaphoreType.DMA((3,))],
        compiler_params=full,
    )(stream_q, stream_k, stream_v)
    halo, w_proj = lax.optimization_barrier((halo, w_proj))
    w_all = lax.all_gather(w_proj.reshape(TOK, 2 * HID), "dp", axis=0, tiled=True)
    halo = lax.ppermute(halo, "dp", [(s, s + 1) for s in range(2 * NY - 1)])
    x1, x2 = pl.pallas_call(
        mix_kernel,
        out_shape=(
            jax.ShapeDtypeStruct((NZ, ROWS, CH), bf),
            jax.ShapeDtypeStruct((CH, TOK), bf),
        ),
        in_specs=hbm(5) + vm(1),
        out_specs=tuple(vm(2)),
        scratch_shapes=[
            pltpu.VMEM((TOK, CH), bf),
            pltpu.VMEM((TOK, CH), bf),
            pltpu.VMEM((TOK, CH), bf),
            pltpu.VMEM((3, 3, CH), f32),
            pltpu.VMEM((1, CH), bf),
            pltpu.SemaphoreType.DMA((5,)),
        ],
        compiler_params=full,
    )(stream_q, stream_k, stream_v, conv_taps, norm_gain.reshape(1, CH), halo)
    x_pos = lax.rem(lax.axis_index("expert"), NX).astype(jnp.int32).reshape(1)
    x2 = to_row_block(x2)
    x1 = spread_z(x1)
    x1, x2 = lax.optimization_barrier((x1, x2))
    x1_parts = spread_x(x1)
    x2 = spread_z(jnp.broadcast_to(x2[None], (NZ, CH, TOK)))
    x1_parts, x2 = lax.optimization_barrier((x1_parts, x2))
    activation, gm = pl.pallas_call(
        forward_kernel,
        out_shape=(
            jax.ShapeDtypeStruct((TOK, HID), bf),
            jax.ShapeDtypeStruct((TOK, 2 * HID), bf),
        ),
        in_specs=sm(1) + vm(5) + hbm(5),
        out_specs=tuple(vm(2)),
        scratch_shapes=[
            pltpu.VMEM((TOK, D), bf),
            pltpu.VMEM((TOK, HID), bf),
            pltpu.VMEM((1, TOK), f32),
            pltpu.VMEM((1, 384), jnp.int32),
            pltpu.VMEM((1, 2), jnp.int32),
            pltpu.VMEM((D, 2 * HID), bf),
            pltpu.SemaphoreType.DMA((5,)),
        ],
        compiler_params=params,
    )(
        x_pos,
        *x1_parts,
        grad_out,
        route_prob.reshape(1, TOK),
        slot_token,
        expert_count,
        w_all,
    )
    gm_all = lax.all_gather(gm, "dp", axis=0, tiled=True)
    x2, _ = lax.optimization_barrier((x2, gm))
    x2_parts = spread_x(x2)
    grad_w = pl.pallas_call(
        weight_kernel,
        out_shape=jax.ShapeDtypeStruct((TOK, 2 * HID), f32),
        in_specs=sm(1) + vm(5) + hbm(1),
        out_specs=vm(1)[0],
        scratch_shapes=[
            pltpu.VMEM((2 * CH, D), bf),
            pltpu.VMEM((D, 2 * HID), bf),
            pltpu.SemaphoreType.DMA((1,)),
        ],
        compiler_params=params,
    )(x_pos, *x2_parts, gm_all)
    return activation, grad_w.reshape(TOK, 2, HID)


def solution(mesh):
    placed = (
        P("dp", "expert"),
        P("dp", "expert"),
        P("dp", "expert"),
        P(None, None, "expert"),
        P("expert"),
        P("dp", None),
        P("dp", None),
        P("dp"),
        P("dp", None, "expert"),
        P("dp", "expert"),
    )
    return jax.shard_map(
        on_device,
        mesh=mesh,
        in_specs=placed,
        out_specs=(P("dp", "expert"), P("dp", None, "expert")),
        check_vma=False,
    )
```

```python
import functools

import jax
import jax.numpy as jnp
from jax import lax
from jax.experimental import pallas as pl
from jax.experimental.pallas import tpu as pltpu
from jax.sharding import PartitionSpec as P

D = 4096
BLOCK = 128
EPS = 1e-06
NZ, NX, NY = 8, 4, 8
TOK, CH, HID = 256, 128, 256
ROWS = TOK + 16
CROWS = CH + 16
VMEM_LIMIT = 48 * 1024 * 1024
AXES = ("dp", "expert")
Y_GROUPS = [[y * 2 + c for y in range(NY)] for c in range(2)]
Z_GROUPS = [[z * NX + x for z in range(NZ)] for x in range(NX)]


def shift_x(value, steps):
    pairs = [
        (d * NZ * NX + z * NX + x, d * NZ * NX + z * NX + (x + steps) % NX)
        for d in range(2 * NY)
        for z in range(NZ)
        for x in range(NX)
    ]
    return lax.ppermute(value, AXES, pairs)


def other_core(value):
    pairs = [(n, (n // (NZ * NX) ^ 1) * NZ * NX + n % (NZ * NX)) for n in range(2 * NY * NZ * NX)]
    return lax.ppermute(value, AXES, pairs)


def to_row_block(value):
    pairs = [
        (i * NZ * NX + j, (j // 2) * NZ * NX + 2 * i + j % 2)
        for i in range(2 * NY)
        for j in range(NZ * NX)
    ]
    return lax.ppermute(value, AXES, pairs)


def spread(copies, axis, groups):
    n, r, c = copies.shape
    return lax.all_to_all(
        copies.reshape(n * r, c), axis, 0, 0, axis_index_groups=groups, tiled=True
    ).reshape(n, r, c)


def spread_z(copies):
    return spread(copies, "expert", Z_GROUPS)


def spread_x(b):
    half = b.shape[0] // 2
    return (b, shift_x(b, 1), shift_x(b, -1), shift_x(b[:half], 2), shift_x(b[half:], -2))


def gathered_blocks(x_ref, parts):
    own, from_left, from_right, low, high = parts
    x = x_ref[0]
    for ref, off, z0 in (
        (own, 0, 0),
        (from_left, NX - 1, 0),
        (from_right, 1, 0),
        (low, 2, 0),
        (high, 2, NZ // 2),
    ):
        xx = lax.rem(x + off, NX)
        for k in range(ref.shape[0]):
            yield ref, k, (z0 + k) * NX + xx


def load_all(pairs, sems):
    copies = [pltpu.make_async_copy(src, dst, sems.at[n]) for n, (src, dst) in enumerate(pairs)]
    for copy in copies:
        copy.start()
    return copies


def pack_kernel(q_ref, k_ref, v_ref, out_ref, sems):
    last = pl.ds(TOK - 16, 16)
    for copy in load_all(
        [(r.at[last], out_ref.at[s]) for s, r in enumerate((q_ref, k_ref, v_ref))], sems
    ):
        copy.wait()


def in_second(slot_ref, count_ref):
    first = (count_ref[0:1, 0:1] + BLOCK - 1) // BLOCK * BLOCK
    slots = slot_ref.shape[1]
    tok = lax.broadcasted_iota(jnp.int32, (TOK, slots), 0)
    place = lax.broadcasted_iota(jnp.int32, (TOK, slots), 1)
    hit = jnp.where((slot_ref[...] == tok) & (place >= first), 1.0, 0.0)
    return jnp.sum(hit, axis=1, keepdims=True)


def diagonal():
    r = lax.broadcasted_iota(jnp.int32, (TOK, TOK), 0)
    c = lax.broadcasted_iota(jnp.int32, (TOK, TOK), 1)
    return r == c


def mix_kernel(
    q_hbm, k_hbm, v_hbm, taps_hbm, gain_hbm, slot_hbm, count_hbm, halo_ref, x1_ref, x2_ref,
    q_ref, k_ref, v_ref, taps_ref, gain_ref, slot_ref, count_ref, sems,
):
    for copy in load_all(
        [
            (q_hbm, q_ref),
            (k_hbm, k_ref),
            (v_hbm, v_ref),
            (taps_hbm, taps_ref),
            (gain_hbm, gain_ref),
            (slot_hbm, slot_ref),
            (count_hbm, count_ref),
        ],
        sems,
    ):
        copy.wait()
    prod = None
    row = lax.broadcasted_iota(jnp.int32, (TOK, CH), 0)
    for s, ref in enumerate((q_ref, k_ref, v_ref)):
        cur = ref[...].astype(jnp.float32)
        before = halo_ref[s].astype(jnp.float32)
        h0, h1 = before[14:15, :], before[15:16, :]
        lag1 = jnp.where(row == 0, h1, pltpu.roll(cur, 1, 0))
        lag2 = jnp.where(row == 0, h0, jnp.where(row == 1, h1, pltpu.roll(cur, 2, 0)))
        conv = (
            taps_ref[s, 0:1, :] * cur + taps_ref[s, 1:2, :] * lag1 + taps_ref[s, 2:3, :] * lag2
        )
        prod = conv if prod is None else prod * conv
    mixed = prod.astype(jnp.bfloat16)
    gain = gain_ref[...].astype(jnp.float32)
    tail = jnp.broadcast_to(gain, (16, CH)).astype(jnp.bfloat16)
    for n in range(NZ):
        x1_ref[n, 0:TOK, :] = mixed
        x1_ref[n, TOK:ROWS, :] = tail
    scaled = mixed.astype(jnp.float32) * gain
    x2_ref[0:CH, :] = scaled.T.astype(jnp.bfloat16)
    second = jnp.sum(
        jnp.where(diagonal(), in_second(slot_ref, count_ref), 0.0), axis=0, keepdims=True
    )
    x2_ref[CH:CROWS, :] = jnp.broadcast_to(second, (16, TOK)).astype(jnp.bfloat16)


def forward_kernel(x_ref, *refs):
    parts = refs[:5]
    sources, (act_ref, gm_ref, xn_ref), held, sems = refs[5:10], refs[10:13], refs[13:18], refs[18]
    g_ref, prob_ref, slot_ref, count_ref, w_ref = held
    copies = load_all(list(zip(sources, held)), sems)
    square = jnp.zeros((TOK, CH), jnp.float32)
    for ref, k, j in gathered_blocks(x_ref, parts):
        m = ref[k, 0:TOK, :].astype(jnp.float32)
        gain = ref[k, TOK : TOK + 16, :].astype(jnp.float32)[0:1, :]
        square = square + m * m
        xn_ref[:, pl.ds(pl.multiple_of(j * CH, CH), CH)] = (m * gain).astype(jnp.bfloat16)
    inv = lax.rsqrt(jnp.sum(square, axis=1, keepdims=True) / D + EPS)
    for copy in copies:
        copy.wait()
    both = jnp.dot(xn_ref[...], w_ref[...], preferred_element_type=jnp.float32)
    second = in_second(slot_ref, count_ref) > 0.5
    prob = jnp.sum(jnp.where(diagonal(), prob_ref[...], 0.0), axis=1, keepdims=True)
    pre = jnp.where(second, both[:, HID:], both[:, :HID]) * inv
    sig = jax.nn.sigmoid(pre)
    act_ref[...] = (prob * pre * sig).astype(jnp.bfloat16)
    grad = g_ref[...].astype(jnp.float32) * prob * sig * (1.0 + pre * (1.0 - sig)) * inv
    grad = grad.astype(jnp.bfloat16)
    for n in range(NY):
        gm_ref[n] = grad


def weight_kernel(x_ref, *refs):
    parts = refs[:5]
    mine_hbm, other_hbm, out_ref, xt_ref, gm_ref, sems = refs[5:]
    copies = load_all([(mine_hbm, gm_ref.at[0]), (other_hbm, gm_ref.at[1])], sems)
    for ref, k, j in gathered_blocks(x_ref, parts):
        i = lax.div(j, 2)
        place = jnp.where(lax.rem(i, 2) == x_ref[1], lax.div(i, 2), NY + lax.div(i, 2))
        rows = pl.ds(pl.multiple_of(lax.rem(j, 2) * CH, CH), CH)
        cols = pl.ds(pl.multiple_of(place * TOK, TOK), TOK)
        second = ref[k, CH:CROWS, :].astype(jnp.float32)[0:1, :]
        block = ref[k, 0:CH, :].astype(jnp.float32)
        xt_ref[0, rows, cols] = (block * (1.0 - second)).astype(jnp.bfloat16)
        xt_ref[1, rows, cols] = (block * second).astype(jnp.bfloat16)
    for copy in copies:
        copy.wait()
    grads = gm_ref[...].reshape(D, HID)
    for e in range(2):
        out_ref[:, e * HID : (e + 1) * HID] = jnp.dot(
            xt_ref[e], grads, preferred_element_type=jnp.float32
        )


def vm(n):
    return [pl.BlockSpec(memory_space=pltpu.VMEM)] * n


def hbm(n):
    return [pl.BlockSpec(memory_space=pltpu.HBM)] * n


def sm(n):
    return [pl.BlockSpec(memory_space=pltpu.SMEM)] * n


def on_device(
    stream_q,
    stream_k,
    stream_v,
    conv_taps,
    norm_gain,
    slot_token,
    expert_count,
    route_prob,
    w_proj,
    grad_out,
):
    params = pltpu.CompilerParams(vmem_limit_bytes=VMEM_LIMIT)
    full = pltpu.CompilerParams(vmem_limit_bytes=56 * 1024 * 1024)
    bf, f32 = jnp.bfloat16, jnp.float32
    halo = pl.pallas_call(
        pack_kernel,
        out_shape=jax.ShapeDtypeStruct((3, 16, CH), bf),
        in_specs=hbm(3),
        out_specs=vm(1)[0],
        scratch_shapes=[pltpu.SemaphoreType.DMA((3,))],
        compiler_params=full,
    )(stream_q, stream_k, stream_v)
    halo, w_proj = lax.optimization_barrier((halo, w_proj))
    w_all = lax.all_gather(w_proj.reshape(TOK, 2 * HID), "dp", axis=0, tiled=True)
    halo = lax.ppermute(halo, "dp", [(s, s + 1) for s in range(2 * NY - 1)])
    x1, x2 = pl.pallas_call(
        mix_kernel,
        out_shape=(
            jax.ShapeDtypeStruct((NZ, ROWS, CH), bf),
            jax.ShapeDtypeStruct((CROWS, TOK), bf),
        ),
        in_specs=hbm(7) + vm(1),
        out_specs=tuple(vm(2)),
        scratch_shapes=[
            pltpu.VMEM((TOK, CH), bf),
            pltpu.VMEM((TOK, CH), bf),
            pltpu.VMEM((TOK, CH), bf),
            pltpu.VMEM((3, 3, CH), f32),
            pltpu.VMEM((1, CH), bf),
            pltpu.VMEM((1, 384), jnp.int32),
            pltpu.VMEM((1, 2), jnp.int32),
            pltpu.SemaphoreType.DMA((7,)),
        ],
        compiler_params=full,
    )(stream_q, stream_k, stream_v, conv_taps, norm_gain.reshape(1, CH), slot_token, expert_count, halo)
    x_pos = jnp.stack([lax.rem(lax.axis_index("expert"), NX), lax.rem(lax.axis_index("dp"), 2)])
    x_pos = x_pos.astype(jnp.int32)
    x2 = to_row_block(x2)
    x1 = spread_z(x1)
    x1, x2 = lax.optimization_barrier((x1, x2))
    x1_parts = spread_x(x1)
    x2 = spread_z(jnp.broadcast_to(x2[None], (NZ, CROWS, TOK)))
    x1_parts, x2 = lax.optimization_barrier((x1_parts, x2))
    activation, gm = pl.pallas_call(
        forward_kernel,
        out_shape=(
            jax.ShapeDtypeStruct((TOK, HID), bf),
            jax.ShapeDtypeStruct((NY, TOK, HID), bf),
        ),
        in_specs=sm(1) + vm(5) + hbm(5),
        out_specs=tuple(vm(2)),
        scratch_shapes=[
            pltpu.VMEM((TOK, D), bf),
            pltpu.VMEM((TOK, HID), bf),
            pltpu.VMEM((1, TOK), f32),
            pltpu.VMEM((1, 384), jnp.int32),
            pltpu.VMEM((1, 2), jnp.int32),
            pltpu.VMEM((D, 2 * HID), bf),
            pltpu.SemaphoreType.DMA((5,)),
        ],
        compiler_params=params,
    )(
        x_pos,
        *x1_parts,
        grad_out,
        route_prob.reshape(1, TOK),
        slot_token,
        expert_count,
        w_all,
    )
    x2, gm = lax.optimization_barrier((x2, gm))
    mine = spread(gm, "dp", Y_GROUPS)
    x2_parts = spread_x(x2)
    mine, x2_parts = lax.optimization_barrier((mine, x2_parts))
    gm_parts = (mine, other_core(mine))
    grad_w = pl.pallas_call(
        weight_kernel,
        out_shape=jax.ShapeDtypeStruct((TOK, 2 * HID), f32),
        in_specs=sm(1) + vm(5) + hbm(2),
        out_specs=vm(1)[0],
        scratch_shapes=[
            pltpu.VMEM((2, 2 * CH, D), bf),
            pltpu.VMEM((2, NY, TOK, HID), bf),
            pltpu.SemaphoreType.DMA((2,)),
        ],
        compiler_params=params,
    )(x_pos, *x2_parts, *gm_parts)
    return activation, grad_w.reshape(TOK, 2, HID)


def solution(mesh):
    placed = (
        P("dp", "expert"),
        P("dp", "expert"),
        P("dp", "expert"),
        P(None, None, "expert"),
        P("expert"),
        P("dp", None),
        P("dp", None),
        P("dp"),
        P("dp", None, "expert"),
        P("dp", "expert"),
    )
    return jax.shard_map(
        on_device,
        mesh=mesh,
        in_specs=placed,
        out_specs=(P("dp", "expert"), P("dp", None, "expert")),
        check_vma=False,
    )
```

```python
import itertools

import jax
import jax.numpy as jnp
from jax import lax
from jax.experimental import pallas as pl
from jax.experimental.pallas import tpu as pltpu
from jax.sharding import PartitionSpec as P

D = 4096
BLOCK = 128
EPS = 1e-06
NZ, NX, NY = 8, 4, 8
TOK, CH, HID = 256, 128, 256
ROWS = TOK + 16
CROWS = CH + 16
HALVES = TOK // CH
VMEM_LIMIT = 40 * 1024 * 1024
AXES = ("dp", "expert")
Y_GROUPS = [[y * 2 + c for y in range(NY)] for c in range(2)]
Z_GROUPS = [[z * NX + x for z in range(NZ)] for x in range(NX)]


def shift_x(value, steps):
    pairs = [
        (d * NZ * NX + z * NX + x, d * NZ * NX + z * NX + (x + steps) % NX)
        for d in range(2 * NY)
        for z in range(NZ)
        for x in range(NX)
    ]
    return lax.ppermute(value, AXES, pairs)


def other_core(value):
    pairs = [(n, (n // (NZ * NX) ^ 1) * NZ * NX + n % (NZ * NX)) for n in range(2 * NY * NZ * NX)]
    return lax.ppermute(value, AXES, pairs)


def to_row_block(value):
    pairs = [
        (i * NZ * NX + j, (j // 2) * NZ * NX + 2 * i + j % 2)
        for i in range(2 * NY)
        for j in range(NZ * NX)
    ]
    return lax.ppermute(value, AXES, pairs)


def spread(copies, axis, groups):
    n, r, c = copies.shape
    return lax.all_to_all(
        copies.reshape(n * r, c), axis, 0, 0, axis_index_groups=groups, tiled=True
    )


def load_all(pairs, sems):
    copies = [pltpu.make_async_copy(src, dst, sems.at[n]) for n, (src, dst) in enumerate(pairs)]
    for copy in copies:
        copy.start()
    return copies


def pack_kernel(q_ref, k_ref, v_ref, out_ref, sems):
    last = pl.ds(TOK - 16, 16)
    for copy in load_all(
        [(r.at[last], out_ref.at[s]) for s, r in enumerate((q_ref, k_ref, v_ref))], sems
    ):
        copy.wait()


def in_second(slot_ref, count_ref):
    first = (count_ref[0:1, 0:1] + BLOCK - 1) // BLOCK * BLOCK
    slots = slot_ref.shape[1]
    tok = lax.broadcasted_iota(jnp.int32, (TOK, slots), 0)
    place = lax.broadcasted_iota(jnp.int32, (TOK, slots), 1)
    hit = jnp.where((slot_ref[...] == tok) & (place >= first), 1.0, 0.0)
    return jnp.sum(hit, axis=1, keepdims=True)


def diagonal():
    r = lax.broadcasted_iota(jnp.int32, (TOK, TOK), 0)
    c = lax.broadcasted_iota(jnp.int32, (TOK, TOK), 1)
    return r == c


def mix_kernel(
    q_hbm, k_hbm, v_hbm, taps_hbm, gain_hbm, slot_hbm, count_hbm, halo_ref, x1_ref, x2_ref,
    q_ref, k_ref, v_ref, taps_ref, gain_ref, slot_ref, count_ref, sems,
):
    for copy in load_all(
        [
            (q_hbm, q_ref),
            (k_hbm, k_ref),
            (v_hbm, v_ref),
            (taps_hbm, taps_ref),
            (gain_hbm, gain_ref),
            (slot_hbm, slot_ref),
            (count_hbm, count_ref),
        ],
        sems,
    ):
        copy.wait()
    prod = None
    row = lax.broadcasted_iota(jnp.int32, (TOK, CH), 0)
    for s, ref in enumerate((q_ref, k_ref, v_ref)):
        cur = ref[...].astype(jnp.float32)
        before = halo_ref[s].astype(jnp.float32)
        h0, h1 = before[14:15, :], before[15:16, :]
        lag1 = jnp.where(row == 0, h1, pltpu.roll(cur, 1, 0))
        lag2 = jnp.where(row == 0, h0, jnp.where(row == 1, h1, pltpu.roll(cur, 2, 0)))
        conv = (
            taps_ref[s, 0:1, :] * cur + taps_ref[s, 1:2, :] * lag1 + taps_ref[s, 2:3, :] * lag2
        )
        prod = conv if prod is None else prod * conv
    mixed = prod.astype(jnp.bfloat16)
    gain = gain_ref[...].astype(jnp.float32)
    tail = jnp.broadcast_to(gain, (16, CH)).astype(jnp.bfloat16)
    for n in range(NZ):
        x1_ref[n, 0:TOK, :] = mixed
        x1_ref[n, TOK:ROWS, :] = tail
    scaled = mixed.astype(jnp.float32) * gain
    turned = scaled.T.astype(jnp.bfloat16)
    second = jnp.sum(
        jnp.where(diagonal(), in_second(slot_ref, count_ref), 0.0), axis=0, keepdims=True
    )
    second = jnp.broadcast_to(second, (16, TOK)).astype(jnp.bfloat16)
    for h in range(HALVES):
        tokens = slice(h * CH, (h + 1) * CH)
        x2_ref[h * CROWS : h * CROWS + CH, :] = turned[:, tokens]
        x2_ref[h * CROWS + CH : (h + 1) * CROWS, :] = second[:, tokens]


def scaled_rows(ref, blocks, first, xn_ref, square):
    for k in range(blocks):
        row = k * ROWS
        m = ref[row : row + TOK, :].astype(jnp.float32)
        gain = ref[row + TOK : row + ROWS, :].astype(jnp.float32)[0:1, :]
        square = square + m * m
        xn_ref[:, (first + k) * CH : (first + k + 1) * CH] = (m * gain).astype(jnp.bfloat16)
    return square


def near_kernel(x_ref, own_ref, left_ref, right_ref, w_hbm, acc_ref, square_ref, xn_ref, w_ref, sems):
    x = x_ref[0]
    copies = load_all(
        [
            (w_hbm.at[:, lax.rem(x + off, NX)], w_ref.at[n])
            for n, off in enumerate((0, NX - 1, 1))
        ],
        sems,
    )
    square = jnp.zeros((TOK, CH), jnp.float32)
    for n, ref in enumerate((own_ref, left_ref, right_ref)):
        square = scaled_rows(ref, NZ, n * NZ, xn_ref, square)
    square_ref[...] = square
    for copy in copies:
        copy.wait()
    acc_ref[...] = jnp.dot(
        xn_ref[...], w_ref[...].reshape(3 * NZ * CH, 2 * HID), preferred_element_type=jnp.float32
    )


def forward_kernel(
    x_ref, low_ref, high_ref, acc_ref, square_ref, g_hbm, prob_hbm, slot_hbm, count_hbm, w_hbm,
    act_ref, gm_ref, xn_ref, g_ref, prob_ref, slot_ref, count_ref, w_ref, sems,
):
    copies = load_all(
        [
            (w_hbm.at[:, lax.rem(x_ref[0] + 2, NX)], w_ref),
            (g_hbm, g_ref),
            (prob_hbm, prob_ref),
            (slot_hbm, slot_ref),
            (count_hbm, count_ref),
        ],
        sems,
    )
    square = scaled_rows(low_ref, NZ // 2, 0, xn_ref, square_ref[...])
    square = scaled_rows(high_ref, NZ // 2, NZ // 2, xn_ref, square)
    inv = lax.rsqrt(jnp.sum(square, axis=1, keepdims=True) / D + EPS)
    for copy in copies:
        copy.wait()
    both = acc_ref[...] + jnp.dot(
        xn_ref[...], w_ref[...].reshape(NZ * CH, 2 * HID), preferred_element_type=jnp.float32
    )
    second = in_second(slot_ref, count_ref) > 0.5
    prob = jnp.sum(jnp.where(diagonal(), prob_ref[...], 0.0), axis=1, keepdims=True)
    pre = jnp.where(second, both[:, HID:], both[:, :HID]) * inv
    sig = jax.nn.sigmoid(pre)
    act_ref[...] = (prob * pre * sig).astype(jnp.bfloat16)
    grad = g_ref[...].astype(jnp.float32) * prob * sig * (1.0 + pre * (1.0 - sig)) * inv
    grad = grad.astype(jnp.bfloat16)
    for n in range(NY):
        gm_ref[n] = grad


def weight_mine_kernel(x_ref, x_hbm, mine_hbm, acc_ref, rest_ref, xt_ref, rows_ref, gm_ref, sems):
    copies = load_all([(x_hbm, rows_ref), (mine_hbm, gm_ref)], sems)
    copies[0].wait()
    half_x = [lax.rem(x_ref[0] + off, NX) for off in (0, NX - 1, 1, 2)]
    for z, n in itertools.product(range(NZ), range(NX)):
        xx = half_x[n]
        rows = pl.ds(pl.multiple_of(lax.rem(xx, 2) * CH, CH), CH)
        side = jnp.where(lax.div(xx, 2) == x_ref[1], 0, 1)
        for h in range(HALVES):
            cols = pl.ds(z * TOK + h * CH, CH)
            top = h * CROWS
            second = rows_ref[z, n, top + CH : top + CROWS, :].astype(jnp.float32)[0:1, :]
            block = rows_ref[z, n, top : top + CH, :].astype(jnp.float32)
            xt_ref[side, 0, rows, cols] = (block * (1.0 - second)).astype(jnp.bfloat16)
            xt_ref[side, 1, rows, cols] = (block * second).astype(jnp.bfloat16)
    copies[1].wait()
    grads = gm_ref[...].reshape(NY * TOK, HID)
    for e in range(2):
        acc_ref[e] = jnp.dot(xt_ref[0, e], grads, preferred_element_type=jnp.float32)
        rest_ref[e] = xt_ref[1, e]


def weight_kernel(acc_ref, rest_ref, other_ref, out_ref):
    grads = other_ref[...].reshape(NY * TOK, HID)
    for e in range(2):
        out_ref[:, e * HID : (e + 1) * HID] = acc_ref[e] + jnp.dot(
            rest_ref[e], grads, preferred_element_type=jnp.float32
        )


def vm(n):
    return [pl.BlockSpec(memory_space=pltpu.VMEM)] * n


def hbm(n):
    return [pl.BlockSpec(memory_space=pltpu.HBM)] * n


def sm(n):
    return [pl.BlockSpec(memory_space=pltpu.SMEM)] * n


def on_device(
    stream_q,
    stream_k,
    stream_v,
    conv_taps,
    norm_gain,
    slot_token,
    expert_count,
    route_prob,
    w_proj,
    grad_out,
):
    params = pltpu.CompilerParams(vmem_limit_bytes=VMEM_LIMIT)
    full = pltpu.CompilerParams(vmem_limit_bytes=56 * 1024 * 1024)
    bf, f32 = jnp.bfloat16, jnp.float32
    halo = pl.pallas_call(
        pack_kernel,
        out_shape=jax.ShapeDtypeStruct((3, 16, CH), bf),
        in_specs=hbm(3),
        out_specs=vm(1)[0],
        scratch_shapes=[pltpu.SemaphoreType.DMA((3,))],
        compiler_params=full,
    )(stream_q, stream_k, stream_v)
    halo, w_proj = lax.optimization_barrier((halo, w_proj))
    w_all = lax.all_gather(w_proj.reshape(TOK, 2 * HID), "dp", axis=0, tiled=True)
    halo = lax.ppermute(halo, "dp", [(s, s + 1) for s in range(2 * NY - 1)])
    x1, x2 = pl.pallas_call(
        mix_kernel,
        out_shape=(
            jax.ShapeDtypeStruct((NZ, ROWS, CH), bf),
            jax.ShapeDtypeStruct((HALVES * CROWS, CH), bf),
        ),
        in_specs=hbm(7) + vm(1),
        out_specs=tuple(vm(2)),
        scratch_shapes=[
            pltpu.VMEM((TOK, CH), bf),
            pltpu.VMEM((TOK, CH), bf),
            pltpu.VMEM((TOK, CH), bf),
            pltpu.VMEM((3, 3, CH), f32),
            pltpu.VMEM((1, CH), bf),
            pltpu.VMEM((1, 384), jnp.int32),
            pltpu.VMEM((1, 2), jnp.int32),
            pltpu.SemaphoreType.DMA((7,)),
        ],
        compiler_params=full,
    )(stream_q, stream_k, stream_v, conv_taps, norm_gain.reshape(1, CH), slot_token, expert_count, halo)
    x_pos = jnp.stack([lax.rem(lax.axis_index("expert"), NX), lax.rem(lax.axis_index("dp"), 2)])
    x_pos = x_pos.astype(jnp.int32)
    x2 = to_row_block(x2)
    x1 = spread(x1, "expert", Z_GROUPS)
    x1, x2 = lax.optimization_barrier((x1, x2))
    rows = NZ * ROWS
    both = jnp.concatenate([x1, x2])
    left, right = shift_x(both, 1), shift_x(both, -1)
    x2_far = shift_x(x2, 2)
    left, right, x2_far = lax.optimization_barrier((left, right, x2_far))
    far = (shift_x(left[: rows // 2], 1), shift_x(right[rows // 2 : rows], -1))
    x2 = jnp.stack([x2, left[rows:], right[rows:], x2_far])
    x2_all = lax.all_gather(x2, "expert", axis=0, axis_index_groups=Z_GROUPS)
    w_all = w_all.reshape(NZ, NX, CH, 2 * HID)
    acc, square = pl.pallas_call(
        near_kernel,
        out_shape=(
            jax.ShapeDtypeStruct((TOK, 2 * HID), f32),
            jax.ShapeDtypeStruct((TOK, CH), f32),
        ),
        in_specs=sm(1) + vm(3) + hbm(1),
        out_specs=tuple(vm(2)),
        scratch_shapes=[
            pltpu.VMEM((TOK, 3 * NZ * CH), bf),
            pltpu.VMEM((3, NZ, CH, 2 * HID), bf),
            pltpu.SemaphoreType.DMA((3,)),
        ],
        compiler_params=params,
        cost_estimate=pl.CostEstimate(flops=800_000_000, bytes_accessed=6_000_000, transcendentals=0),
    )(x_pos, x1, left, right, w_all)
    activation, gm = pl.pallas_call(
        forward_kernel,
        out_shape=(
            jax.ShapeDtypeStruct((TOK, HID), bf),
            jax.ShapeDtypeStruct((NY, TOK, HID), bf),
        ),
        in_specs=sm(1) + vm(4) + hbm(5),
        out_specs=tuple(vm(2)),
        scratch_shapes=[
            pltpu.VMEM((TOK, NZ * CH), bf),
            pltpu.VMEM((TOK, HID), bf),
            pltpu.VMEM((1, TOK), f32),
            pltpu.VMEM((1, 384), jnp.int32),
            pltpu.VMEM((1, 2), jnp.int32),
            pltpu.VMEM((NZ, CH, 2 * HID), bf),
            pltpu.SemaphoreType.DMA((5,)),
        ],
        compiler_params=params,
    )(
        x_pos,
        *far,
        acc,
        square,
        grad_out,
        route_prob.reshape(1, TOK),
        slot_token,
        expert_count,
        w_all,
    )
    mine = spread(gm, "dp", Y_GROUPS).reshape(NY, TOK, HID)
    other = other_core(mine)
    acc, rest = pl.pallas_call(
        weight_mine_kernel,
        out_shape=(
            jax.ShapeDtypeStruct((2, 2 * CH, HID), f32),
            jax.ShapeDtypeStruct((2, 2 * CH, NY * TOK), bf),
        ),
        in_specs=sm(1) + hbm(2),
        out_specs=tuple(vm(2)),
        scratch_shapes=[
            pltpu.VMEM((2, 2, 2 * CH, NY * TOK), bf),
            pltpu.VMEM((NZ, NX, HALVES * CROWS, CH), bf),
            pltpu.VMEM((NY, TOK, HID), bf),
            pltpu.SemaphoreType.DMA((2,)),
        ],
        compiler_params=params,
        cost_estimate=pl.CostEstimate(flops=500_000_000, bytes_accessed=6_000_000, transcendentals=0),
    )(x_pos, x2_all, mine)
    grad_w = pl.pallas_call(
        weight_kernel,
        out_shape=jax.ShapeDtypeStruct((TOK, 2 * HID), f32),
        in_specs=vm(3),
        out_specs=vm(1)[0],
        compiler_params=params,
    )(acc, rest, other)
    return activation, grad_w.reshape(TOK, 2, HID)


def solution(mesh):
    placed = (
        P("dp", "expert"),
        P("dp", "expert"),
        P("dp", "expert"),
        P(None, None, "expert"),
        P("expert"),
        P("dp", None),
        P("dp", None),
        P("dp"),
        P("dp", None, "expert"),
        P("dp", "expert"),
    )
    return jax.shard_map(
        on_device,
        mesh=mesh,
        in_specs=placed,
        out_specs=(P("dp", "expert"), P("dp", None, "expert")),
        check_vma=False,
    )
```

```python
import itertools

import jax
import jax.numpy as jnp
from jax import lax
from jax.experimental import pallas as pl
from jax.experimental.pallas import tpu as pltpu
from jax.sharding import PartitionSpec as P

D = 4096
BLOCK = 128
EPS = 1e-06
NZ, NX, NY = 8, 4, 8
TOK, CH, HID = 256, 128, 256
ROWS = TOK + 16
CROWS = CH + 16
HALVES = TOK // CH
VMEM_LIMIT = 40 * 1024 * 1024
AXES = ("dp", "expert")
Y_GROUPS = [[y * 2 + c for y in range(NY)] for c in range(2)]
Z_GROUPS = [[z * NX + x for z in range(NZ)] for x in range(NX)]


def shift_x(value, steps):
    pairs = [
        (d * NZ * NX + z * NX + x, d * NZ * NX + z * NX + (x + steps) % NX)
        for d in range(2 * NY)
        for z in range(NZ)
        for x in range(NX)
    ]
    return lax.ppermute(value, AXES, pairs)


def other_core(value):
    pairs = [(n, (n // (NZ * NX) ^ 1) * NZ * NX + n % (NZ * NX)) for n in range(2 * NY * NZ * NX)]
    return lax.ppermute(value, AXES, pairs)


def to_row_block(value):
    pairs = [
        (i * NZ * NX + j, (j // 2) * NZ * NX + 2 * i + j % 2)
        for i in range(2 * NY)
        for j in range(NZ * NX)
    ]
    return lax.ppermute(value, AXES, pairs)


def spread(copies, axis, groups):
    n, r, c = copies.shape
    return lax.all_to_all(
        copies.reshape(n * r, c), axis, 0, 0, axis_index_groups=groups, tiled=True
    )


def load_all(pairs, sems):
    copies = [pltpu.make_async_copy(src, dst, sems.at[n]) for n, (src, dst) in enumerate(pairs)]
    for copy in copies:
        copy.start()
    return copies


def pack_kernel(q_ref, k_ref, v_ref, out_ref, sems):
    last = pl.ds(TOK - 16, 16)
    for copy in load_all(
        [(r.at[last], out_ref.at[s]) for s, r in enumerate((q_ref, k_ref, v_ref))], sems
    ):
        copy.wait()


def in_second(slot_ref, count_ref):
    first = (count_ref[0:1, 0:1] + BLOCK - 1) // BLOCK * BLOCK
    slots = slot_ref.shape[1]
    tok = lax.broadcasted_iota(jnp.int32, (TOK, slots), 0)
    place = lax.broadcasted_iota(jnp.int32, (TOK, slots), 1)
    hit = jnp.where((slot_ref[...] == tok) & (place >= first), 1.0, 0.0)
    return jnp.sum(hit, axis=1, keepdims=True)


def diagonal():
    r = lax.broadcasted_iota(jnp.int32, (TOK, TOK), 0)
    c = lax.broadcasted_iota(jnp.int32, (TOK, TOK), 1)
    return r == c


def mix_kernel(
    q_hbm, k_hbm, v_hbm, taps_hbm, gain_hbm, slot_hbm, count_hbm, halo_ref, x1_ref, x2_ref,
    q_ref, k_ref, v_ref, taps_ref, gain_ref, slot_ref, count_ref, sems,
):
    for copy in load_all(
        [
            (q_hbm, q_ref),
            (k_hbm, k_ref),
            (v_hbm, v_ref),
            (taps_hbm, taps_ref),
            (gain_hbm, gain_ref),
            (slot_hbm, slot_ref),
            (count_hbm, count_ref),
        ],
        sems,
    ):
        copy.wait()
    prod = None
    row = lax.broadcasted_iota(jnp.int32, (TOK, CH), 0)
    for s, ref in enumerate((q_ref, k_ref, v_ref)):
        cur = ref[...].astype(jnp.float32)
        before = halo_ref[s].astype(jnp.float32)
        h0, h1 = before[14:15, :], before[15:16, :]
        lag1 = jnp.where(row == 0, h1, pltpu.roll(cur, 1, 0))
        lag2 = jnp.where(row == 0, h0, jnp.where(row == 1, h1, pltpu.roll(cur, 2, 0)))
        conv = (
            taps_ref[s, 0:1, :] * cur + taps_ref[s, 1:2, :] * lag1 + taps_ref[s, 2:3, :] * lag2
        )
        prod = conv if prod is None else prod * conv
    mixed = prod.astype(jnp.bfloat16)
    gain = gain_ref[...].astype(jnp.float32)
    tail = jnp.broadcast_to(gain, (16, CH)).astype(jnp.bfloat16)
    for n in range(NZ):
        x1_ref[n, 0:TOK, :] = mixed
        x1_ref[n, TOK:ROWS, :] = tail
    scaled = mixed.astype(jnp.float32) * gain
    turned = scaled.T.astype(jnp.bfloat16)
    second = jnp.sum(
        jnp.where(diagonal(), in_second(slot_ref, count_ref), 0.0), axis=0, keepdims=True
    )
    second = jnp.broadcast_to(second, (16, TOK)).astype(jnp.bfloat16)
    for h in range(HALVES):
        tokens = slice(h * CH, (h + 1) * CH)
        x2_ref[h * CROWS : h * CROWS + CH, :] = turned[:, tokens]
        x2_ref[h * CROWS + CH : (h + 1) * CROWS, :] = second[:, tokens]


def scaled_rows(ref, blocks, first, xn_ref, square):
    for k in range(blocks):
        row = k * ROWS
        m = ref[row : row + TOK, :].astype(jnp.float32)
        gain = ref[row + TOK : row + ROWS, :].astype(jnp.float32)[0:1, :]
        square = square + m * m
        xn_ref[:, (first + k) * CH : (first + k + 1) * CH] = (m * gain).astype(jnp.bfloat16)
    return square


def near_kernel(x_ref, own_ref, left_ref, right_ref, w_hbm, acc_ref, square_ref, xn_ref, w_ref, sems):
    x = x_ref[0]
    copies = load_all(
        [
            (w_hbm.at[:, lax.rem(x + off, NX)], w_ref.at[n])
            for n, off in enumerate((0, NX - 1, 1))
        ],
        sems,
    )
    square = jnp.zeros((TOK, CH), jnp.float32)
    for n, ref in enumerate((own_ref, left_ref, right_ref)):
        square = scaled_rows(ref, NZ, n * NZ, xn_ref, square)
    square_ref[...] = square
    for copy in copies:
        copy.wait()
    acc_ref[...] = jnp.dot(
        xn_ref[...], w_ref[...].reshape(3 * NZ * CH, 2 * HID), preferred_element_type=jnp.float32
    )


def forward_kernel(
    x_ref, low_ref, high_ref, acc_ref, square_ref, g_hbm, prob_hbm, slot_hbm, count_hbm, w_hbm,
    act_ref, gm_ref, xn_ref, g_ref, prob_ref, slot_ref, count_ref, w_ref, sems,
):
    copies = load_all(
        [
            (w_hbm.at[:, lax.rem(x_ref[0] + 2, NX)], w_ref),
            (g_hbm, g_ref),
            (prob_hbm, prob_ref),
            (slot_hbm, slot_ref),
            (count_hbm, count_ref),
        ],
        sems,
    )
    square = scaled_rows(low_ref, NZ // 2, 0, xn_ref, square_ref[...])
    square = scaled_rows(high_ref, NZ // 2, NZ // 2, xn_ref, square)
    inv = lax.rsqrt(jnp.sum(square, axis=1, keepdims=True) / D + EPS)
    for copy in copies:
        copy.wait()
    both = acc_ref[...] + jnp.dot(
        xn_ref[...], w_ref[...].reshape(NZ * CH, 2 * HID), preferred_element_type=jnp.float32
    )
    second = in_second(slot_ref, count_ref) > 0.5
    prob = jnp.sum(jnp.where(diagonal(), prob_ref[...], 0.0), axis=1, keepdims=True)
    pre = jnp.where(second, both[:, HID:], both[:, :HID]) * inv
    sig = jax.nn.sigmoid(pre)
    act_ref[...] = (prob * pre * sig).astype(jnp.bfloat16)
    grad = g_ref[...].astype(jnp.float32) * prob * sig * (1.0 + pre * (1.0 - sig)) * inv
    grad = grad.astype(jnp.bfloat16)
    for n in range(NY):
        gm_ref[n] = grad


def weight_mine_kernel(x_ref, rows_ref, gm_ref, acc_ref, xt_ref):
    half_x = [lax.rem(x_ref[0] + off, NX) for off in (0, NX - 1, 1, 2)]
    for z, n in itertools.product(range(NZ), range(NX)):
        xx = half_x[n]
        rows = pl.ds(pl.multiple_of(lax.rem(xx, 2) * CH, CH), CH)
        side = jnp.where(lax.div(xx, 2) == x_ref[1], 0, 1)
        for h in range(HALVES):
            cols = pl.ds(z * TOK + h * CH, CH)
            top = h * CROWS
            second = jnp.broadcast_to(rows_ref[z, n, top + CH : top + CROWS, :][0:1, :], (CH, CH))
            block = rows_ref[z, n, top : top + CH, :]
            masked = block * second
            xt_ref[side, 0, rows, cols] = block - masked
            xt_ref[side, 1, rows, cols] = masked
    grads = gm_ref[...].reshape(NY * TOK, HID)
    for e in range(2):
        acc_ref[e] = jnp.dot(xt_ref[0, e], grads, preferred_element_type=jnp.float32)


def weight_kernel(acc_ref, rest_ref, other_ref, out_ref):
    grads = other_ref[...].reshape(NY * TOK, HID)
    for e in range(2):
        out_ref[:, e, :] = acc_ref[e] + jnp.dot(
            rest_ref[1, e], grads, preferred_element_type=jnp.float32
        )


def vm(n):
    return [pl.BlockSpec(memory_space=pltpu.VMEM)] * n


def hbm(n):
    return [pl.BlockSpec(memory_space=pltpu.HBM)] * n


def sm(n):
    return [pl.BlockSpec(memory_space=pltpu.SMEM)] * n


def on_device(
    stream_q,
    stream_k,
    stream_v,
    conv_taps,
    norm_gain,
    slot_token,
    expert_count,
    route_prob,
    w_proj,
    grad_out,
):
    params = pltpu.CompilerParams(vmem_limit_bytes=VMEM_LIMIT)
    full = pltpu.CompilerParams(vmem_limit_bytes=56 * 1024 * 1024)
    bf, f32 = jnp.bfloat16, jnp.float32
    halo = pl.pallas_call(
        pack_kernel,
        out_shape=jax.ShapeDtypeStruct((3, 16, CH), bf),
        in_specs=hbm(3),
        out_specs=vm(1)[0],
        scratch_shapes=[pltpu.SemaphoreType.DMA((3,))],
        compiler_params=full,
    )(stream_q, stream_k, stream_v)
    halo, w_proj = lax.optimization_barrier((halo, w_proj))
    w_all = lax.all_gather(w_proj.reshape(TOK, 2 * HID), "dp", axis=0, tiled=True)
    halo = lax.ppermute(halo, "dp", [(s, s + 1) for s in range(2 * NY - 1)])
    x1, x2 = pl.pallas_call(
        mix_kernel,
        out_shape=(
            jax.ShapeDtypeStruct((NZ, ROWS, CH), bf),
            jax.ShapeDtypeStruct((HALVES * CROWS, CH), bf),
        ),
        in_specs=hbm(7) + vm(1),
        out_specs=tuple(vm(2)),
        scratch_shapes=[
            pltpu.VMEM((TOK, CH), bf),
            pltpu.VMEM((TOK, CH), bf),
            pltpu.VMEM((TOK, CH), bf),
            pltpu.VMEM((3, 3, CH), f32),
            pltpu.VMEM((1, CH), bf),
            pltpu.VMEM((1, 384), jnp.int32),
            pltpu.VMEM((1, 2), jnp.int32),
            pltpu.SemaphoreType.DMA((7,)),
        ],
        compiler_params=full,
    )(stream_q, stream_k, stream_v, conv_taps, norm_gain.reshape(1, CH), slot_token, expert_count, halo)
    x_pos = jnp.stack([lax.rem(lax.axis_index("expert"), NX), lax.rem(lax.axis_index("dp"), 2)])
    x_pos = x_pos.astype(jnp.int32)
    x2 = to_row_block(x2)
    x1 = spread(x1, "expert", Z_GROUPS)
    x1, x2 = lax.optimization_barrier((x1, x2))
    rows = NZ * ROWS
    both = jnp.concatenate([x1, x2])
    left, right = shift_x(both, 1), shift_x(both, -1)
    x2_far = shift_x(x2, 2)
    left, right, x2_far = lax.optimization_barrier((left, right, x2_far))
    far = (shift_x(left[: rows // 2], 1), shift_x(right[rows // 2 : rows], -1))
    x2 = jnp.stack([x2, left[rows:], right[rows:], x2_far])
    x2_all = lax.all_gather(x2, "expert", axis=0, axis_index_groups=Z_GROUPS)
    w_all = w_all.reshape(NZ, NX, CH, 2 * HID)
    acc, square = pl.pallas_call(
        near_kernel,
        out_shape=(
            jax.ShapeDtypeStruct((TOK, 2 * HID), f32),
            jax.ShapeDtypeStruct((TOK, CH), f32),
        ),
        in_specs=sm(1) + vm(3) + hbm(1),
        out_specs=tuple(vm(2)),
        scratch_shapes=[
            pltpu.VMEM((TOK, 3 * NZ * CH), bf),
            pltpu.VMEM((3, NZ, CH, 2 * HID), bf),
            pltpu.SemaphoreType.DMA((3,)),
        ],
        compiler_params=params,
        cost_estimate=pl.CostEstimate(flops=800_000_000, bytes_accessed=6_000_000, transcendentals=0),
    )(x_pos, x1, left, right, w_all)
    activation, gm = pl.pallas_call(
        forward_kernel,
        out_shape=(
            jax.ShapeDtypeStruct((TOK, HID), bf),
            jax.ShapeDtypeStruct((NY, TOK, HID), bf),
        ),
        in_specs=sm(1) + vm(4) + hbm(5),
        out_specs=tuple(vm(2)),
        scratch_shapes=[
            pltpu.VMEM((TOK, NZ * CH), bf),
            pltpu.VMEM((TOK, HID), bf),
            pltpu.VMEM((1, TOK), f32),
            pltpu.VMEM((1, 384), jnp.int32),
            pltpu.VMEM((1, 2), jnp.int32),
            pltpu.VMEM((NZ, CH, 2 * HID), bf),
            pltpu.SemaphoreType.DMA((5,)),
        ],
        compiler_params=params,
    )(
        x_pos,
        *far,
        acc,
        square,
        grad_out,
        route_prob.reshape(1, TOK),
        slot_token,
        expert_count,
        w_all,
    )
    mine = spread(gm, "dp", Y_GROUPS).reshape(NY, TOK, HID)
    other = other_core(mine)
    acc, rest = pl.pallas_call(
        weight_mine_kernel,
        out_shape=(
            jax.ShapeDtypeStruct((2, 2 * CH, HID), f32),
            jax.ShapeDtypeStruct((2, 2, 2 * CH, NY * TOK), bf),
        ),
        in_specs=sm(1) + vm(2),
        out_specs=tuple(vm(2)),
        compiler_params=params,
        cost_estimate=pl.CostEstimate(flops=500_000_000, bytes_accessed=6_000_000, transcendentals=0),
    )(x_pos, x2_all, mine)
    grad_w = pl.pallas_call(
        weight_kernel,
        out_shape=jax.ShapeDtypeStruct((TOK, 2, HID), f32),
        in_specs=vm(3),
        out_specs=vm(1)[0],
        compiler_params=params,
    )(acc, rest, other)
    return activation, grad_w


def solution(mesh):
    placed = (
        P("dp", "expert"),
        P("dp", "expert"),
        P("dp", "expert"),
        P(None, None, "expert"),
        P("expert"),
        P("dp", None),
        P("dp", None),
        P("dp"),
        P("dp", None, "expert"),
        P("dp", "expert"),
    )
    return jax.shard_map(
        on_device,
        mesh=mesh,
        in_specs=placed,
        out_specs=(P("dp", "expert"), P("dp", None, "expert")),
        check_vma=False,
    )
```

```python
import itertools

import jax
import jax.numpy as jnp
from jax import lax
from jax.experimental import pallas as pl
from jax.experimental.pallas import tpu as pltpu
from jax.sharding import PartitionSpec as P

D = 4096
BLOCK = 128
EPS = 1e-06
NZ, NX, NY = 8, 4, 8
TOK, CH, HID = 256, 128, 256
ROWS = TOK + 16
CROWS = CH + 16
HALVES = TOK // CH
VMEM_LIMIT = 40 * 1024 * 1024
AXES = ("dp", "expert")
Y_GROUPS = [[y * 2 + c for y in range(NY)] for c in range(2)]
Z_GROUPS = [[z * NX + x for z in range(NZ)] for x in range(NX)]


def shift_x(value, steps):
    pairs = [
        (d * NZ * NX + z * NX + x, d * NZ * NX + z * NX + (x + steps) % NX)
        for d in range(2 * NY)
        for z in range(NZ)
        for x in range(NX)
    ]
    return lax.ppermute(value, AXES, pairs)


def other_core(value):
    pairs = [(n, (n // (NZ * NX) ^ 1) * NZ * NX + n % (NZ * NX)) for n in range(2 * NY * NZ * NX)]
    return lax.ppermute(value, AXES, pairs)


def to_row_block(value):
    pairs = [
        (i * NZ * NX + j, (j // 2) * NZ * NX + 2 * i + j % 2)
        for i in range(2 * NY)
        for j in range(NZ * NX)
    ]
    return lax.ppermute(value, AXES, pairs)


def spread(copies, axis, groups):
    n, r, c = copies.shape
    return lax.all_to_all(
        copies.reshape(n * r, c), axis, 0, 0, axis_index_groups=groups, tiled=True
    )


def load_all(pairs, sems):
    copies = [pltpu.make_async_copy(src, dst, sems.at[n]) for n, (src, dst) in enumerate(pairs)]
    for copy in copies:
        copy.start()
    return copies


def pack_kernel(q_ref, k_ref, v_ref, out_ref, sems):
    last = pl.ds(TOK - 16, 16)
    for copy in load_all(
        [(r.at[last], out_ref.at[s]) for s, r in enumerate((q_ref, k_ref, v_ref))], sems
    ):
        copy.wait()


def in_second(slot_ref, count_ref):
    first = (count_ref[0:1, 0:1] + BLOCK - 1) // BLOCK * BLOCK
    slots = slot_ref.shape[1]
    tok = lax.broadcasted_iota(jnp.int32, (TOK, slots), 0)
    place = lax.broadcasted_iota(jnp.int32, (TOK, slots), 1)
    hit = jnp.where((slot_ref[...] == tok) & (place >= first), 1.0, 0.0)
    return jnp.sum(hit, axis=1, keepdims=True)


def diagonal():
    r = lax.broadcasted_iota(jnp.int32, (TOK, TOK), 0)
    c = lax.broadcasted_iota(jnp.int32, (TOK, TOK), 1)
    return r == c


def mix_kernel(
    q_hbm, k_hbm, v_hbm, taps_hbm, slot_hbm, count_hbm, gain_ref, halo_ref, x1_ref, x2_ref,
    q_ref, k_ref, v_ref, taps_ref, slot_ref, count_ref, sems,
):
    for copy in load_all(
        [
            (q_hbm, q_ref),
            (k_hbm, k_ref),
            (v_hbm, v_ref),
            (taps_hbm, taps_ref),
            (slot_hbm, slot_ref),
            (count_hbm, count_ref),
        ],
        sems,
    ):
        copy.wait()
    prod = None
    row = lax.broadcasted_iota(jnp.int32, (TOK, CH), 0)
    for s, ref in enumerate((q_ref, k_ref, v_ref)):
        cur = ref[...].astype(jnp.float32)
        before = halo_ref[s].astype(jnp.float32)
        h0, h1 = before[14:15, :], before[15:16, :]
        lag1 = jnp.where(row == 0, h1, pltpu.roll(cur, 1, 0))
        lag2 = jnp.where(row == 0, h0, jnp.where(row == 1, h1, pltpu.roll(cur, 2, 0)))
        conv = (
            taps_ref[s, 0:1, :] * cur + taps_ref[s, 1:2, :] * lag1 + taps_ref[s, 2:3, :] * lag2
        )
        prod = conv if prod is None else prod * conv
    mixed = prod.astype(jnp.bfloat16)
    gain = gain_ref[...].astype(jnp.float32)
    tail = jnp.broadcast_to(gain, (16, CH)).astype(jnp.bfloat16)
    for n in range(NZ):
        x1_ref[n, 0:TOK, :] = mixed
        x1_ref[n, TOK:ROWS, :] = tail
    scaled = mixed.astype(jnp.float32) * gain
    turned = scaled.T.astype(jnp.bfloat16)
    second = jnp.sum(
        jnp.where(diagonal(), in_second(slot_ref, count_ref), 0.0), axis=0, keepdims=True
    )
    second = jnp.broadcast_to(second, (16, TOK)).astype(jnp.bfloat16)
    for h in range(HALVES):
        tokens = slice(h * CH, (h + 1) * CH)
        x2_ref[h * CROWS : h * CROWS + CH, :] = turned[:, tokens]
        x2_ref[h * CROWS + CH : (h + 1) * CROWS, :] = second[:, tokens]


def scaled_rows(ref, blocks, first, xn_ref, square):
    for k in range(blocks):
        row = k * ROWS
        m = ref[row : row + TOK, :].astype(jnp.float32)
        gain = ref[row + TOK : row + ROWS, :].astype(jnp.float32)[0:1, :]
        square = square + m * m
        xn_ref[:, (first + k) * CH : (first + k + 1) * CH] = (m * gain).astype(jnp.bfloat16)
    return square


def near_kernel(x_ref, own_ref, left_ref, right_ref, w_hbm, acc_ref, square_ref, xn_ref, w_ref, sems):
    x = x_ref[0]
    copies = load_all(
        [
            (w_hbm.at[:, lax.rem(x + off, NX)], w_ref.at[n])
            for n, off in enumerate((0, NX - 1, 1))
        ],
        sems,
    )
    square = jnp.zeros((TOK, CH), jnp.float32)
    for n, ref in enumerate((own_ref, left_ref, right_ref)):
        square = scaled_rows(ref, NZ, n * NZ, xn_ref, square)
    square_ref[...] = square
    for copy in copies:
        copy.wait()
    acc_ref[...] = jnp.dot(
        xn_ref[...], w_ref[...].reshape(3 * NZ * CH, 2 * HID), preferred_element_type=jnp.float32
    )


def forward_kernel(
    x_ref, low_ref, high_ref, acc_ref, square_ref, g_hbm, prob_hbm, slot_hbm, count_hbm, w_hbm,
    act_ref, gm_ref, xn_ref, g_ref, prob_ref, slot_ref, count_ref, w_ref, sems,
):
    copies = load_all(
        [
            (w_hbm.at[:, lax.rem(x_ref[0] + 2, NX)], w_ref),
            (g_hbm, g_ref),
            (prob_hbm, prob_ref),
            (slot_hbm, slot_ref),
            (count_hbm, count_ref),
        ],
        sems,
    )
    square = scaled_rows(low_ref, NZ // 2, 0, xn_ref, square_ref[...])
    square = scaled_rows(high_ref, NZ // 2, NZ // 2, xn_ref, square)
    inv = lax.rsqrt(jnp.sum(square, axis=1, keepdims=True) / D + EPS)
    for copy in copies:
        copy.wait()
    both = acc_ref[...] + jnp.dot(
        xn_ref[...], w_ref[...].reshape(NZ * CH, 2 * HID), preferred_element_type=jnp.float32
    )
    second = in_second(slot_ref, count_ref) > 0.5
    prob = jnp.sum(jnp.where(diagonal(), prob_ref[...], 0.0), axis=1, keepdims=True)
    pre = jnp.where(second, both[:, HID:], both[:, :HID]) * inv
    sig = jax.nn.sigmoid(pre)
    act_ref[...] = (prob * pre * sig).astype(jnp.bfloat16)
    grad = g_ref[...].astype(jnp.float32) * prob * sig * (1.0 + pre * (1.0 - sig)) * inv
    grad = grad.astype(jnp.bfloat16)
    for n in range(NY):
        gm_ref[n] = grad


def weight_mine_kernel(x_ref, rows_ref, gm_ref, acc_ref, xt_ref):
    half_x = [lax.rem(x_ref[0] + off, NX) for off in (0, NX - 1, 1, 2)]
    for z, n in itertools.product(range(NZ), range(NX)):
        xx = half_x[n]
        rows = pl.ds(pl.multiple_of(lax.rem(xx, 2) * CH, CH), CH)
        side = jnp.where(lax.div(xx, 2) == x_ref[1], 0, 1)
        for h in range(HALVES):
            cols = pl.ds(z * TOK + h * CH, CH)
            top = h * CROWS
            second = jnp.broadcast_to(rows_ref[z, n, top + CH : top + CROWS, :][0:1, :], (CH, CH))
            block = rows_ref[z, n, top : top + CH, :]
            masked = block * second
            xt_ref[side, 0, rows, cols] = block - masked
            xt_ref[side, 1, rows, cols] = masked
    grads = gm_ref[...].reshape(NY * TOK, HID)
    for e in range(2):
        acc_ref[e] = jnp.dot(xt_ref[0, e], grads, preferred_element_type=jnp.float32)


def weight_kernel(acc_ref, rest_ref, other_ref, out_ref):
    grads = other_ref[...].reshape(NY * TOK, HID)
    for e in range(2):
        out_ref[:, e, :] = acc_ref[e] + jnp.dot(
            rest_ref[1, e], grads, preferred_element_type=jnp.float32
        )


def vm(n):
    return [pl.BlockSpec(memory_space=pltpu.VMEM)] * n


def hbm(n):
    return [pl.BlockSpec(memory_space=pltpu.HBM)] * n


def sm(n):
    return [pl.BlockSpec(memory_space=pltpu.SMEM)] * n


def on_device(
    stream_q,
    stream_k,
    stream_v,
    conv_taps,
    norm_gain,
    slot_token,
    expert_count,
    route_prob,
    w_proj,
    grad_out,
):
    params = pltpu.CompilerParams(vmem_limit_bytes=VMEM_LIMIT)
    full = pltpu.CompilerParams(vmem_limit_bytes=56 * 1024 * 1024)
    bf, f32 = jnp.bfloat16, jnp.float32
    halo = pl.pallas_call(
        pack_kernel,
        out_shape=jax.ShapeDtypeStruct((3, 16, CH), bf),
        in_specs=hbm(3),
        out_specs=vm(1)[0],
        scratch_shapes=[pltpu.SemaphoreType.DMA((3,))],
        compiler_params=full,
    )(stream_q, stream_k, stream_v)
    halo, w_proj = lax.optimization_barrier((halo, w_proj))
    w_all = lax.all_gather(w_proj.reshape(TOK, 2 * HID), "dp", axis=0, tiled=True)
    halo = lax.ppermute(halo, "dp", [(s, s + 1) for s in range(2 * NY - 1)])
    x1, x2 = pl.pallas_call(
        mix_kernel,
        out_shape=(
            jax.ShapeDtypeStruct((NZ, ROWS, CH), bf),
            jax.ShapeDtypeStruct((HALVES * CROWS, CH), bf),
        ),
        in_specs=hbm(6) + vm(2),
        out_specs=tuple(vm(2)),
        scratch_shapes=[
            pltpu.VMEM((TOK, CH), bf),
            pltpu.VMEM((TOK, CH), bf),
            pltpu.VMEM((TOK, CH), bf),
            pltpu.VMEM((3, 3, CH), f32),
            pltpu.VMEM((1, 384), jnp.int32),
            pltpu.VMEM((1, 2), jnp.int32),
            pltpu.SemaphoreType.DMA((6,)),
        ],
        compiler_params=full,
    )(stream_q, stream_k, stream_v, conv_taps, slot_token, expert_count, norm_gain.reshape(1, CH), halo)
    x_pos = jnp.stack([lax.rem(lax.axis_index("expert"), NX), lax.rem(lax.axis_index("dp"), 2)])
    x_pos = x_pos.astype(jnp.int32)
    x2 = to_row_block(x2)
    x1 = spread(x1, "expert", Z_GROUPS)
    x1, x2 = lax.optimization_barrier((x1, x2))
    rows = NZ * ROWS
    both = jnp.concatenate([x1, x2])
    left, right = shift_x(both, 1), shift_x(both, -1)
    x2_far = shift_x(x2, 2)
    left, right, x2_far = lax.optimization_barrier((left, right, x2_far))
    far = (shift_x(left[: rows // 2], 1), shift_x(right[rows // 2 : rows], -1))
    x2 = jnp.stack([x2, left[rows:], right[rows:], x2_far])
    x2_all = lax.all_gather(x2, "expert", axis=0, axis_index_groups=Z_GROUPS)
    w_all = w_all.reshape(NZ, NX, CH, 2 * HID)
    acc, square = pl.pallas_call(
        near_kernel,
        out_shape=(
            jax.ShapeDtypeStruct((TOK, 2 * HID), f32),
            jax.ShapeDtypeStruct((TOK, CH), f32),
        ),
        in_specs=sm(1) + vm(3) + hbm(1),
        out_specs=tuple(vm(2)),
        scratch_shapes=[
            pltpu.VMEM((TOK, 3 * NZ * CH), bf),
            pltpu.VMEM((3, NZ, CH, 2 * HID), bf),
            pltpu.SemaphoreType.DMA((3,)),
        ],
        compiler_params=params,
        cost_estimate=pl.CostEstimate(flops=800_000_000, bytes_accessed=6_000_000, transcendentals=0),
    )(x_pos, x1, left, right, w_all)
    activation, gm = pl.pallas_call(
        forward_kernel,
        out_shape=(
            jax.ShapeDtypeStruct((TOK, HID), bf),
            jax.ShapeDtypeStruct((NY, TOK, HID), bf),
        ),
        in_specs=sm(1) + vm(4) + hbm(5),
        out_specs=tuple(vm(2)),
        scratch_shapes=[
            pltpu.VMEM((TOK, NZ * CH), bf),
            pltpu.VMEM((TOK, HID), bf),
            pltpu.VMEM((1, TOK), f32),
            pltpu.VMEM((1, 384), jnp.int32),
            pltpu.VMEM((1, 2), jnp.int32),
            pltpu.VMEM((NZ, CH, 2 * HID), bf),
            pltpu.SemaphoreType.DMA((5,)),
        ],
        compiler_params=params,
    )(
        x_pos,
        *far,
        acc,
        square,
        grad_out,
        route_prob.reshape(1, TOK),
        slot_token,
        expert_count,
        w_all,
    )
    mine = spread(gm, "dp", Y_GROUPS).reshape(NY, TOK, HID)
    other = other_core(mine)
    acc, rest = pl.pallas_call(
        weight_mine_kernel,
        out_shape=(
            jax.ShapeDtypeStruct((2, 2 * CH, HID), f32),
            jax.ShapeDtypeStruct((2, 2, 2 * CH, NY * TOK), bf),
        ),
        in_specs=sm(1) + vm(2),
        out_specs=tuple(vm(2)),
        compiler_params=params,
        cost_estimate=pl.CostEstimate(flops=500_000_000, bytes_accessed=6_000_000, transcendentals=0),
    )(x_pos, x2_all, mine)
    grad_w = pl.pallas_call(
        weight_kernel,
        out_shape=jax.ShapeDtypeStruct((TOK, 2, HID), f32),
        in_specs=vm(3),
        out_specs=vm(1)[0],
        compiler_params=params,
    )(acc, rest, other)
    return activation, grad_w


def solution(mesh):
    placed = (
        P("dp", "expert"),
        P("dp", "expert"),
        P("dp", "expert"),
        P(None, None, "expert"),
        P("expert"),
        P("dp", None),
        P("dp", None),
        P("dp"),
        P("dp", None, "expert"),
        P("dp", "expert"),
    )
    return jax.shard_map(
        on_device,
        mesh=mesh,
        in_specs=placed,
        out_specs=(P("dp", "expert"), P("dp", None, "expert")),
        check_vma=False,
    )
```

```python
import itertools

import jax
import jax.numpy as jnp
from jax import lax
from jax.experimental import pallas as pl
from jax.experimental.pallas import tpu as pltpu
from jax.sharding import PartitionSpec as P

D = 4096
BLOCK = 128
EPS = 1e-06
NZ, NX, NY = 8, 4, 8
TOK, CH, HID = 256, 128, 256
ROWS = TOK + 16
CROWS = CH + 16
HALVES = TOK // CH
VMEM_LIMIT = 40 * 1024 * 1024
AXES = ("dp", "expert")
Y_GROUPS = [[y * 2 + c for y in range(NY)] for c in range(2)]
Z_GROUPS = [[z * NX + x for z in range(NZ)] for x in range(NX)]


def shift_x(value, steps):
    pairs = [
        (d * NZ * NX + z * NX + x, d * NZ * NX + z * NX + (x + steps) % NX)
        for d in range(2 * NY)
        for z in range(NZ)
        for x in range(NX)
    ]
    return lax.ppermute(value, AXES, pairs)


def other_core(value):
    pairs = [(n, (n // (NZ * NX) ^ 1) * NZ * NX + n % (NZ * NX)) for n in range(2 * NY * NZ * NX)]
    return lax.ppermute(value, AXES, pairs)


def to_row_block(value):
    pairs = [
        (i * NZ * NX + j, (j // 2) * NZ * NX + 2 * i + j % 2)
        for i in range(2 * NY)
        for j in range(NZ * NX)
    ]
    return lax.ppermute(value, AXES, pairs)


def spread(copies, axis, groups):
    n, r, c = copies.shape
    return lax.all_to_all(
        copies.reshape(n * r, c), axis, 0, 0, axis_index_groups=groups, tiled=True
    )


def load_all(pairs, sems):
    copies = [pltpu.make_async_copy(src, dst, sems.at[n]) for n, (src, dst) in enumerate(pairs)]
    for copy in copies:
        copy.start()
    return copies


def pack_kernel(q_ref, k_ref, v_ref, out_ref, sems):
    last = pl.ds(TOK - 16, 16)
    for copy in load_all(
        [(r.at[last], out_ref.at[s]) for s, r in enumerate((q_ref, k_ref, v_ref))], sems
    ):
        copy.wait()


def in_second(slot_ref, count_ref):
    first = (count_ref[0:1, 0:1] + BLOCK - 1) // BLOCK * BLOCK
    slots = slot_ref.shape[1]
    tok = lax.broadcasted_iota(jnp.int32, (TOK, slots), 0)
    place = lax.broadcasted_iota(jnp.int32, (TOK, slots), 1)
    hit = jnp.where((slot_ref[...] == tok) & (place >= first), 1.0, 0.0)
    return jnp.sum(hit, axis=1, keepdims=True)


def diagonal():
    r = lax.broadcasted_iota(jnp.int32, (TOK, TOK), 0)
    c = lax.broadcasted_iota(jnp.int32, (TOK, TOK), 1)
    return r == c


def route_kernel(slot_ref, count_ref, out_ref):
    second = jnp.sum(
        jnp.where(diagonal(), in_second(slot_ref, count_ref), 0.0), axis=0, keepdims=True
    )
    out_ref[...] = jnp.broadcast_to(second, (16, TOK)).astype(jnp.bfloat16)


def mix_kernel(
    q_hbm, k_hbm, v_hbm, taps_hbm, second_hbm, gain_ref, halo_ref, x1_ref, x2_ref,
    q_ref, k_ref, v_ref, taps_ref, second_ref, sems,
):
    for copy in load_all(
        [
            (q_hbm, q_ref),
            (k_hbm, k_ref),
            (v_hbm, v_ref),
            (taps_hbm, taps_ref),
            (second_hbm, second_ref),
        ],
        sems,
    ):
        copy.wait()
    prod = None
    row = lax.broadcasted_iota(jnp.int32, (TOK, CH), 0)
    for s, ref in enumerate((q_ref, k_ref, v_ref)):
        cur = ref[...].astype(jnp.float32)
        before = halo_ref[s].astype(jnp.float32)
        h0, h1 = before[14:15, :], before[15:16, :]
        lag1 = jnp.where(row == 0, h1, pltpu.roll(cur, 1, 0))
        lag2 = jnp.where(row == 0, h0, jnp.where(row == 1, h1, pltpu.roll(cur, 2, 0)))
        conv = (
            taps_ref[s, 0:1, :] * cur + taps_ref[s, 1:2, :] * lag1 + taps_ref[s, 2:3, :] * lag2
        )
        prod = conv if prod is None else prod * conv
    mixed = prod.astype(jnp.bfloat16)
    gain = gain_ref[...].astype(jnp.float32)
    tail = jnp.broadcast_to(gain, (16, CH)).astype(jnp.bfloat16)
    for n in range(NZ):
        x1_ref[n, 0:TOK, :] = mixed
        x1_ref[n, TOK:ROWS, :] = tail
    scaled = mixed.astype(jnp.float32) * gain
    turned = scaled.T.astype(jnp.bfloat16)
    second = second_ref[...]
    for h in range(HALVES):
        tokens = slice(h * CH, (h + 1) * CH)
        x2_ref[h * CROWS : h * CROWS + CH, :] = turned[:, tokens]
        x2_ref[h * CROWS + CH : (h + 1) * CROWS, :] = second[:, tokens]


def scaled_rows(ref, blocks, first, xn_ref, square):
    for k in range(blocks):
        row = k * ROWS
        m = ref[row : row + TOK, :].astype(jnp.float32)
        gain = ref[row + TOK : row + ROWS, :].astype(jnp.float32)[0:1, :]
        square = square + m * m
        xn_ref[:, (first + k) * CH : (first + k + 1) * CH] = (m * gain).astype(jnp.bfloat16)
    return square


def near_kernel(x_ref, own_ref, left_ref, right_ref, w_hbm, acc_ref, square_ref, xn_ref, w_ref, sems):
    x = x_ref[0]
    copies = load_all(
        [
            (w_hbm.at[:, lax.rem(x + off, NX)], w_ref.at[n])
            for n, off in enumerate((0, NX - 1, 1))
        ],
        sems,
    )
    square = jnp.zeros((TOK, CH), jnp.float32)
    for n, ref in enumerate((own_ref, left_ref, right_ref)):
        square = scaled_rows(ref, NZ, n * NZ, xn_ref, square)
    square_ref[...] = square
    for copy in copies:
        copy.wait()
    acc_ref[...] = jnp.dot(
        xn_ref[...], w_ref[...].reshape(3 * NZ * CH, 2 * HID), preferred_element_type=jnp.float32
    )


def forward_kernel(
    x_ref, low_ref, high_ref, acc_ref, square_ref, g_hbm, prob_hbm, slot_hbm, count_hbm, w_hbm,
    act_ref, gm_ref, xn_ref, g_ref, prob_ref, slot_ref, count_ref, w_ref, sems,
):
    copies = load_all(
        [
            (w_hbm.at[:, lax.rem(x_ref[0] + 2, NX)], w_ref),
            (g_hbm, g_ref),
            (prob_hbm, prob_ref),
            (slot_hbm, slot_ref),
            (count_hbm, count_ref),
        ],
        sems,
    )
    square = scaled_rows(low_ref, NZ // 2, 0, xn_ref, square_ref[...])
    square = scaled_rows(high_ref, NZ // 2, NZ // 2, xn_ref, square)
    inv = lax.rsqrt(jnp.sum(square, axis=1, keepdims=True) / D + EPS)
    for copy in copies:
        copy.wait()
    both = acc_ref[...] + jnp.dot(
        xn_ref[...], w_ref[...].reshape(NZ * CH, 2 * HID), preferred_element_type=jnp.float32
    )
    second = in_second(slot_ref, count_ref) > 0.5
    prob = jnp.sum(jnp.where(diagonal(), prob_ref[...], 0.0), axis=1, keepdims=True)
    pre = jnp.where(second, both[:, HID:], both[:, :HID]) * inv
    sig = jax.nn.sigmoid(pre)
    act_ref[...] = (prob * pre * sig).astype(jnp.bfloat16)
    grad = g_ref[...].astype(jnp.float32) * prob * sig * (1.0 + pre * (1.0 - sig)) * inv
    grad = grad.astype(jnp.bfloat16)
    for n in range(NY):
        gm_ref[n] = grad


def weight_mine_kernel(x_ref, rows_ref, gm_ref, acc_ref, xt_ref):
    half_x = [lax.rem(x_ref[0] + off, NX) for off in (0, NX - 1, 1, 2)]
    for z, n in itertools.product(range(NZ), range(NX)):
        xx = half_x[n]
        rows = pl.ds(pl.multiple_of(lax.rem(xx, 2) * CH, CH), CH)
        side = jnp.where(lax.div(xx, 2) == x_ref[1], 0, 1)
        for h in range(HALVES):
            cols = pl.ds(z * TOK + h * CH, CH)
            top = h * CROWS
            second = jnp.broadcast_to(rows_ref[z, n, top + CH : top + CROWS, :][0:1, :], (CH, CH))
            block = rows_ref[z, n, top : top + CH, :]
            masked = block * second
            xt_ref[side, 0, rows, cols] = block - masked
            xt_ref[side, 1, rows, cols] = masked
    grads = gm_ref[...].reshape(NY * TOK, HID)
    for e in range(2):
        acc_ref[e] = jnp.dot(xt_ref[0, e], grads, preferred_element_type=jnp.float32)


def weight_kernel(acc_ref, rest_ref, other_ref, out_ref):
    grads = other_ref[...].reshape(NY * TOK, HID)
    for e in range(2):
        out_ref[:, e, :] = acc_ref[e] + jnp.dot(
            rest_ref[1, e], grads, preferred_element_type=jnp.float32
        )


def vm(n):
    return [pl.BlockSpec(memory_space=pltpu.VMEM)] * n


def hbm(n):
    return [pl.BlockSpec(memory_space=pltpu.HBM)] * n


def sm(n):
    return [pl.BlockSpec(memory_space=pltpu.SMEM)] * n


def on_device(
    stream_q,
    stream_k,
    stream_v,
    conv_taps,
    norm_gain,
    slot_token,
    expert_count,
    route_prob,
    w_proj,
    grad_out,
):
    params = pltpu.CompilerParams(vmem_limit_bytes=VMEM_LIMIT)
    full = pltpu.CompilerParams(vmem_limit_bytes=56 * 1024 * 1024)
    bf, f32 = jnp.bfloat16, jnp.float32
    halo = pl.pallas_call(
        pack_kernel,
        out_shape=jax.ShapeDtypeStruct((3, 16, CH), bf),
        in_specs=hbm(3),
        out_specs=vm(1)[0],
        scratch_shapes=[pltpu.SemaphoreType.DMA((3,))],
        compiler_params=full,
    )(stream_q, stream_k, stream_v)
    halo, w_proj = lax.optimization_barrier((halo, w_proj))
    w_all = lax.all_gather(w_proj.reshape(TOK, 2 * HID), "dp", axis=0, tiled=True)
    second = pl.pallas_call(
        route_kernel,
        out_shape=jax.ShapeDtypeStruct((16, TOK), bf),
        in_specs=vm(2),
        out_specs=vm(1)[0],
        compiler_params=full,
    )(slot_token, expert_count)
    halo = lax.ppermute(halo, "dp", [(s, s + 1) for s in range(2 * NY - 1)])
    x1, x2 = pl.pallas_call(
        mix_kernel,
        out_shape=(
            jax.ShapeDtypeStruct((NZ, ROWS, CH), bf),
            jax.ShapeDtypeStruct((HALVES * CROWS, CH), bf),
        ),
        in_specs=hbm(5) + vm(2),
        out_specs=tuple(vm(2)),
        scratch_shapes=[
            pltpu.VMEM((TOK, CH), bf),
            pltpu.VMEM((TOK, CH), bf),
            pltpu.VMEM((TOK, CH), bf),
            pltpu.VMEM((3, 3, CH), f32),
            pltpu.VMEM((16, TOK), bf),
            pltpu.SemaphoreType.DMA((5,)),
        ],
        compiler_params=full,
    )(stream_q, stream_k, stream_v, conv_taps, second, norm_gain.reshape(1, CH), halo)
    x_pos = jnp.stack([lax.rem(lax.axis_index("expert"), NX), lax.rem(lax.axis_index("dp"), 2)])
    x_pos = x_pos.astype(jnp.int32)
    x2 = to_row_block(x2)
    x1 = spread(x1, "expert", Z_GROUPS)
    x1, x2 = lax.optimization_barrier((x1, x2))
    rows = NZ * ROWS
    both = jnp.concatenate([x1, x2])
    left, right = shift_x(both, 1), shift_x(both, -1)
    x2_far = shift_x(x2, 2)
    left, right, x2_far = lax.optimization_barrier((left, right, x2_far))
    far = (shift_x(left[: rows // 2], 1), shift_x(right[rows // 2 : rows], -1))
    x2 = jnp.stack([x2, left[rows:], right[rows:], x2_far])
    x2_all = lax.all_gather(x2, "expert", axis=0, axis_index_groups=Z_GROUPS)
    w_all = w_all.reshape(NZ, NX, CH, 2 * HID)
    acc, square = pl.pallas_call(
        near_kernel,
        out_shape=(
            jax.ShapeDtypeStruct((TOK, 2 * HID), f32),
            jax.ShapeDtypeStruct((TOK, CH), f32),
        ),
        in_specs=sm(1) + vm(3) + hbm(1),
        out_specs=tuple(vm(2)),
        scratch_shapes=[
            pltpu.VMEM((TOK, 3 * NZ * CH), bf),
            pltpu.VMEM((3, NZ, CH, 2 * HID), bf),
            pltpu.SemaphoreType.DMA((3,)),
        ],
        compiler_params=params,
        cost_estimate=pl.CostEstimate(flops=800_000_000, bytes_accessed=6_000_000, transcendentals=0),
    )(x_pos, x1, left, right, w_all)
    activation, gm = pl.pallas_call(
        forward_kernel,
        out_shape=(
            jax.ShapeDtypeStruct((TOK, HID), bf),
            jax.ShapeDtypeStruct((NY, TOK, HID), bf),
        ),
        in_specs=sm(1) + vm(4) + hbm(5),
        out_specs=tuple(vm(2)),
        scratch_shapes=[
            pltpu.VMEM((TOK, NZ * CH), bf),
            pltpu.VMEM((TOK, HID), bf),
            pltpu.VMEM((1, TOK), f32),
            pltpu.VMEM((1, 384), jnp.int32),
            pltpu.VMEM((1, 2), jnp.int32),
            pltpu.VMEM((NZ, CH, 2 * HID), bf),
            pltpu.SemaphoreType.DMA((5,)),
        ],
        compiler_params=params,
    )(
        x_pos,
        *far,
        acc,
        square,
        grad_out,
        route_prob.reshape(1, TOK),
        slot_token,
        expert_count,
        w_all,
    )
    mine = spread(gm, "dp", Y_GROUPS).reshape(NY, TOK, HID)
    other = other_core(mine)
    acc, rest = pl.pallas_call(
        weight_mine_kernel,
        out_shape=(
            jax.ShapeDtypeStruct((2, 2 * CH, HID), f32),
            jax.ShapeDtypeStruct((2, 2, 2 * CH, NY * TOK), bf),
        ),
        in_specs=sm(1) + vm(2),
        out_specs=tuple(vm(2)),
        compiler_params=params,
        cost_estimate=pl.CostEstimate(flops=500_000_000, bytes_accessed=6_000_000, transcendentals=0),
    )(x_pos, x2_all, mine)
    grad_w = pl.pallas_call(
        weight_kernel,
        out_shape=jax.ShapeDtypeStruct((TOK, 2, HID), f32),
        in_specs=vm(3),
        out_specs=vm(1)[0],
        compiler_params=params,
    )(acc, rest, other)
    return activation, grad_w


def solution(mesh):
    placed = (
        P("dp", "expert"),
        P("dp", "expert"),
        P("dp", "expert"),
        P(None, None, "expert"),
        P("expert"),
        P("dp", None),
        P("dp", None),
        P("dp"),
        P("dp", None, "expert"),
        P("dp", "expert"),
    )
    return jax.shard_map(
        on_device,
        mesh=mesh,
        in_specs=placed,
        out_specs=(P("dp", "expert"), P("dp", None, "expert")),
        check_vma=False,
    )
```
